256 devices in a mesh: pool: 32 (over x, z), ctx: 8 (over y, core).
Axes of the slice: x: 4, y: 4, z: 8, core: 2. Of those that a mesh axis runs over, the one named last changes fastest.
Arguments:
- query_nope: bfloat16 [32, 512, 4096], P('pool', 'ctx'), may hold values from -6 to 6
- query_rope: bfloat16 [32, 512, 2048], P('pool', 'ctx'), may hold values from -600 to 600
- suffix_latent: bfloat16 [32, 512, 512], P('pool', 'ctx'), may hold values from -6 to 6
- suffix_rope: bfloat16 [32, 32768], P('pool', 'ctx'), may hold values from -6 to 6
- absorb_key: bfloat16 [32, 128, 512], replicated, may hold values from -0.5 to 0.5
- absorb_value: bfloat16 [32, 512, 128], replicated, may hold values from -0.25 to 0.25
- pool_latent: bfloat16 [32, 8, 32, 8, 512], P('pool', 'ctx'), may hold values from -6 to 6
- pool_rope: bfloat16 [32, 8, 32, 512], P('pool', 'ctx'), may hold values from -6 to 6
- pool_scale: bfloat16 [32, 8, 32, 8], P('pool', 'ctx'), may hold values from 0.25 to 2
- prefix_tokens: int32 [32], replicated, may hold values from 256 to 2048, as said below
- block_owner: int32 [32, 8, 32], replicated, may hold values from 0 to 31, as said below
- block_slot: int32 [32, 8, 32], replicated, may hold values from 0 to 31, as said below
- write_owner: int32 [32, 8, 8], replicated, may hold values from 0 to 31, as said below
- write_slot: int32 [32, 8, 8], replicated, may hold values from 0 to 7, as said below
Outputs:
- attended: bfloat16 [32, 512, 4096], P('pool', 'ctx')
- written_latent: bfloat16 [32, 8, 8, 8, 512], P('pool', 'ctx')
- written_rope: bfloat16 [32, 8, 8, 512], P('pool', 'ctx')
- written_scale: bfloat16 [32, 8, 8, 8], P('pool', 'ctx')
The draws below stay inside these ranges and needn't reach their ends.
Inputs may be any that keep to these rules, and one draw needn't show every extreme that they name: `prefix_tokens`: multiples of 8; some request has the longest prefix and some the shortest. `block_owner`: for one request and ctx index, every owner keeps exactly 1 of the 32 blocks. `block_slot`: different blocks at one owner and ctx index have different slots. `write_owner`: the 8 new blocks of one request at one ctx index go to different owners; every owner receives exactly 8 new blocks at each ctx index. `write_slot`: new blocks at one owner and ctx index have different slots.
All inputs are finite; a program needn't handle non-finite values.
Results may differ from the reference program's by a relative error of at most 0.011.
Values may be sent and summed in bfloat16 or wider, within the bound.
No kernel may reach another device: no remote copies, remote signals or barrier semaphores. Data moves between devices by JAX's collectives and lax.ppermute only.
A program may use at most 128 MiB of HBM per device.

```python
import math
import jax
import jax.numpy as jnp
from jax import lax

LAT = 512
ROPE = 64
NOPE = 128
VDIM = 128
HEADS = 32
BLOCK = 8
BPC = 32
OWNERS = 32
REQS = 32
GROUP = 512
NEWB = 8
PBLOCKS = 256
N_CTX = 8


def rotary_base(key):
    keys_rope = jax.random.truncated_normal(jax.random.fold_in(key, 11), -6.0, 6.0, (REQS, GROUP, ROPE))
    query_base = jax.random.truncated_normal(jax.random.fold_in(key, 12), -6.0, 6.0, (REQS, GROUP, HEADS * ROPE))
    return (keys_rope, query_base)


def draw_suffix_rope(key, part):
    keys_rope, query_base = rotary_base(key)
    return keys_rope.reshape(REQS, GROUP * ROPE).astype(jnp.bfloat16)


def draw_query_rope(key, part):
    keys_rope, query_base = rotary_base(key)
    return query_base.astype(jnp.bfloat16)


def draw_prefix_tokens(key, part):
    key = jax.random.fold_in(key, 31)
    counts = jax.random.randint(jax.random.fold_in(key, 1), (REQS,), PBLOCKS // 8, PBLOCKS + 1)
    order = jax.random.permutation(jax.random.fold_in(key, 2), REQS)
    counts = counts.at[order[0]].set(PBLOCKS).at[order[1]].set(PBLOCKS // 8)
    return (counts * BLOCK).astype(jnp.int32)


def block_layout(key):
    owner_keys = jax.random.split(jax.random.fold_in(key, 41), REQS * N_CTX)
    rows = jax.vmap(lambda single: jax.random.permutation(single, OWNERS))(owner_keys).reshape(REQS, N_CTX, OWNERS)
    owner = rows[:, :, jnp.arange(BPC) % OWNERS]
    slot_keys = jax.random.split(jax.random.fold_in(key, 42), OWNERS * N_CTX)
    shuffles = jax.vmap(lambda single: jax.random.permutation(single, BPC))(slot_keys).reshape(OWNERS, N_CTX, BPC)
    rank = jnp.arange(BPC) // OWNERS
    position = jnp.arange(REQS)[:, None, None] * (BPC // OWNERS) + rank[None, None, :]
    slot = shuffles[owner, jnp.arange(N_CTX)[None, :, None], position]
    return (owner.astype(jnp.int32), slot.astype(jnp.int32))


def draw_block_owner(key, part):
    owner, slot = block_layout(key)
    return owner


def draw_block_slot(key, part):
    owner, slot = block_layout(key)
    return slot


def write_layout(key):
    shifts = jax.vmap(lambda single: jax.random.permutation(single, REQS))(jax.random.split(jax.random.fold_in(key, 51), N_CTX))
    targets = jax.vmap(lambda single: jax.random.permutation(single, OWNERS))(jax.random.split(jax.random.fold_in(key, 52), N_CTX))
    position = (jnp.transpose(shifts)[:, :, None] + jnp.arange(NEWB)[None, None, :]) % OWNERS
    owner = targets[jnp.arange(N_CTX)[None, :, None], position]
    shuffles = jax.vmap(lambda single: jax.random.permutation(single, NEWB))(jax.random.split(jax.random.fold_in(key, 53), OWNERS * N_CTX)).reshape(OWNERS, N_CTX, NEWB)
    slot = shuffles[owner, jnp.arange(N_CTX)[None, :, None], jnp.arange(NEWB)[None, None, :]]
    return (owner.astype(jnp.int32), slot.astype(jnp.int32))


def draw_write_owner(key, part):
    owner, slot = write_layout(key)
    return owner


def draw_write_slot(key, part):
    owner, slot = write_layout(key)
    return slot


def steps_of(rng, extent, pieces, smallest, largest):
    loudness = 1.0
    for axis_at, parts in pieces:
        draws = jax.random.uniform(jax.random.fold_in(jax.random.fold_in(rng, 6), axis_at), (parts,), jnp.float32, smallest / len(pieces), largest / len(pieces))
        loudness = loudness * jnp.repeat(jnp.exp(draws), extent[axis_at] // parts).reshape((-1,) + (1,) * (len(extent) - 1 - axis_at))
    return loudness


def gaussian(key, extent, width, most, pieces=(), dtype=jnp.bfloat16):
    gain = steps_of(key, extent, pieces, -0.22, 0.18) if pieces else 1.0
    values = jax.random.normal(key, extent, jnp.float32) * width * gain
    return jnp.minimum(jnp.maximum(values, -most), most).astype(dtype)


def setup_inputs(seed: int = 0) -> dict:
    arg_keys = jax.random.split(jax.random.key(seed), 15)
    query_nope = gaussian(arg_keys[0], (REQS, GROUP, HEADS * NOPE), 1.0, 6.0, ((0, 32), (1, 8)))
    query_rope = draw_query_rope(jax.random.fold_in(arg_keys[14], 71), 0)
    suffix_latent = gaussian(arg_keys[2], (REQS, GROUP, LAT), 1.0, 6.0, ((0, 32), (1, 8)))
    suffix_rope = draw_suffix_rope(jax.random.fold_in(arg_keys[14], 71), 0)
    absorb_key = gaussian(arg_keys[4], (HEADS, NOPE, LAT), NOPE ** -0.5, 0.5)
    absorb_value = gaussian(arg_keys[5], (HEADS, LAT, VDIM), LAT ** -0.5, 0.25)
    pool_latent = gaussian(arg_keys[6], (OWNERS, N_CTX, BPC, BLOCK, LAT), 1.0, 6.0, ((0, 32), (1, 8)))
    pool_rope = gaussian(arg_keys[7], (OWNERS, N_CTX, BPC, BLOCK * ROPE), 1.0, 6.0, ((0, 32), (1, 8)))
    pool_scale = jnp.clip(jnp.exp(math.log(2.0) - 2.0794415 * jax.random.uniform(arg_keys[8], (OWNERS, N_CTX, BPC, BLOCK), jnp.float32) ** steps_of(arg_keys[8], (OWNERS, N_CTX, BPC, BLOCK), ((0, 32), (1, 8)), -0.2, 0.2)), 0.25, 2.0).astype(jnp.bfloat16)
    prefix_tokens = draw_prefix_tokens(jax.random.fold_in(arg_keys[14], 71), 0)
    block_owner = draw_block_owner(jax.random.fold_in(arg_keys[14], 71), 0)
    block_slot = draw_block_slot(jax.random.fold_in(arg_keys[14], 71), 0)
    write_owner = draw_write_owner(jax.random.fold_in(arg_keys[14], 71), 0)
    write_slot = draw_write_slot(jax.random.fold_in(arg_keys[14], 71), 0)
    return {"query_nope": query_nope, "query_rope": query_rope, "suffix_latent": suffix_latent, "suffix_rope": suffix_rope, "absorb_key": absorb_key, "absorb_value": absorb_value, "pool_latent": pool_latent, "pool_rope": pool_rope, "pool_scale": pool_scale, "prefix_tokens": prefix_tokens, "block_owner": block_owner, "block_slot": block_slot, "write_owner": write_owner, "write_slot": write_slot}


neg_large = -1.0e30
quant_top = 4.0
quant_eps = 1e-6


def dequantize(values, ropes, scales):
    factor = scales.astype(jnp.float32)[..., None]
    keys = (values.astype(jnp.float32) * factor).astype(jnp.bfloat16)
    shaped = ropes.reshape(ropes.shape[:-1] + (BLOCK, ROPE)).astype(jnp.float32)
    key_rope = (shaped * factor).astype(jnp.bfloat16)
    keys = lax.optimization_barrier(keys)
    key_rope = lax.optimization_barrier(key_rope)
    return keys.reshape(-1, LAT), key_rope.reshape(-1, ROPE)


def quantize(latent, rotary):
    latent_full = latent.astype(jnp.float32)
    rotary_full = rotary.astype(jnp.float32)
    magnitude = jnp.maximum(jnp.max(jnp.abs(latent_full), axis=-1), jnp.max(jnp.abs(rotary_full), axis=-1))
    token_scale = ((magnitude + quant_eps) / quant_top).astype(jnp.bfloat16)
    factor = token_scale.astype(jnp.float32)[..., None]
    return (latent_full / factor).astype(jnp.bfloat16), (rotary_full / factor).astype(jnp.bfloat16), token_scale


def reference(query_nope, query_rope, suffix_latent, suffix_rope, absorb_key, absorb_value, pool_latent, pool_rope, pool_scale, prefix_tokens, block_owner, block_slot, write_owner, write_slot):
    columns = jnp.arange(N_CTX)[:, None]
    score_scale = (NOPE + ROPE) ** -0.5
    starts = (jnp.arange(BPC)[None, :] * N_CTX + columns) * BLOCK
    positions = jnp.arange(GROUP)
    causal = positions[None, :] <= positions[:, None]
    key_weight = absorb_key.astype(jnp.float32)
    value_weight = absorb_value.astype(jnp.float32)

    def one_request(request):
        owners = block_owner[request]
        slots = block_slot[request]
        keys_lat, keys_rope = dequantize(pool_latent[owners, columns, slots], pool_rope[owners, columns, slots], pool_scale[owners, columns, slots])
        live = jnp.repeat((starts < prefix_tokens[request]).reshape(-1), BLOCK)
        all_lat = jnp.concatenate([keys_lat, suffix_latent[request]], axis=0)
        all_rope = jnp.concatenate([keys_rope, suffix_rope[request].reshape(GROUP, ROPE)], axis=0)
        visible = jnp.concatenate([jnp.broadcast_to(live[None, :], (GROUP, live.shape[0])), causal], axis=1)[:, None, :]
        absorbed = jnp.einsum("thn,hnl->thl", query_nope[request].reshape(GROUP, HEADS, NOPE).astype(jnp.float32), key_weight).astype(jnp.bfloat16)
        absorbed = lax.optimization_barrier(absorbed).astype(jnp.float32)
        rotary = query_rope[request].reshape(GROUP, HEADS, ROPE).astype(jnp.float32)
        all_lat_full = all_lat.astype(jnp.float32)
        scores = jnp.einsum("thl,kl->thk", absorbed, all_lat_full) + jnp.einsum("thr,kr->thk", rotary, all_rope.astype(jnp.float32))
        scores = jnp.where(visible, scores * score_scale, neg_large)
        row_top = jnp.max(scores, axis=2, keepdims=True)
        expo = jnp.where(visible, jnp.exp(scores - row_top), 0.0)
        total = jnp.sum(expo, axis=2)
        weights = lax.optimization_barrier(expo.astype(jnp.bfloat16)).astype(jnp.float32)
        mixed = jnp.einsum("thk,kl->thl", weights, all_lat_full) / total[..., None]
        mixed = lax.optimization_barrier(mixed.astype(jnp.bfloat16)).astype(jnp.float32)
        result = jnp.einsum("thl,hlv->thv", mixed, value_weight)
        return result.astype(jnp.bfloat16).reshape(GROUP, HEADS * VDIM)

    attended = lax.map(one_request, jnp.arange(REQS))
    code_lat, code_rope, token_scale = quantize(suffix_latent, suffix_rope.reshape(REQS, GROUP, ROPE))
    column_index = jnp.arange(N_CTX)[None, :, None]
    written_latent = jnp.zeros((OWNERS, N_CTX, NEWB, BLOCK, LAT), jnp.bfloat16).at[write_owner, column_index, write_slot].set(code_lat.reshape(REQS, N_CTX, NEWB, BLOCK, LAT))
    written_rope = jnp.zeros((OWNERS, N_CTX, NEWB, BLOCK * ROPE), jnp.bfloat16).at[write_owner, column_index, write_slot].set(code_rope.reshape(REQS, N_CTX, NEWB, BLOCK * ROPE))
    written_scale = jnp.zeros((OWNERS, N_CTX, NEWB, BLOCK), jnp.bfloat16).at[write_owner, column_index, write_slot].set(token_scale.reshape(REQS, N_CTX, NEWB, BLOCK))
    return attended, written_latent, written_rope, written_scale
```

```python
import functools

import jax
import jax.numpy as jnp
from jax import lax
from jax.experimental import pallas as pl
from jax.experimental.pallas import tpu as pltpu
from jax.sharding import PartitionSpec as P

HIDDEN = -1e30
QUANT_TOP = 4.0
QUANT_EPS = 1e-06
MIB = 1 << 20

F32 = jnp.float32
BF16 = jnp.bfloat16
VMEM = pl.BlockSpec(memory_space=pltpu.VMEM)
SMEM = pl.BlockSpec(memory_space=pltpu.SMEM)


def iota(shape, axis):
    return lax.broadcasted_iota(jnp.int32, shape, axis)


def dot(a, b):
    return jnp.dot(a, b, preferred_element_type=F32)


def dot_nt(a, b):
    return lax.dot_general(a, b, (((1,), (1,)), ((), ())), preferred_element_type=F32)


def fold_matrix(block, rope, lanes):
    shape = (block * rope, lanes)
    return (iota(shape, 0) % rope == iota(shape, 1)).astype(F32).astype(BF16)


def pick_column(table, column):
    return jnp.sum(jnp.where(iota(table.shape, 1) == column, table, 0), axis=1)


def pack_kernel(
    ids, latent, ropes, scales, sfx_latent, sfx_rope, prefix, owners, slots, targets, message, suffix
):
    own, column = ids[0], ids[1]
    count, block, width = latent.shape
    rope = ropes.shape[1] // block
    ctx = owners.shape[1]
    tokens = sfx_latent.shape[0]
    tail = message.shape[2] - width
    rows = 2 * block * count
    fold = fold_matrix(block, rope, tail)

    cube = (count, block, block)
    factor = jnp.broadcast_to(scales[...].astype(F32)[:, None, :], cube)
    factor = jnp.sum(jnp.where(iota(cube, 1) == iota(cube, 2), factor, 0.0), axis=2, keepdims=True)
    keys = (latent[...].astype(F32) * factor).reshape(count * block, width).astype(BF16)
    wide = (count, block, block * rope)
    spread = jnp.broadcast_to(ropes[...].astype(F32)[:, None, :], wide) * factor
    spread = jnp.where(iota(wide, 2) // rope == iota(wide, 1), spread, 0.0)
    key_tail = dot(spread.reshape(count * block, block * rope).astype(BF16), fold).astype(BF16)

    own_latent = sfx_latent[...].astype(F32)
    pieces = []
    for g in range(tokens // block):
        piece = sfx_rope[:, g * block * rope : (g + 1) * block * rope].astype(F32)
        piece = jnp.broadcast_to(piece, (block, block * rope))
        pieces.append(jnp.where(iota(piece.shape, 1) // rope == iota(piece.shape, 0), piece, 0.0))
    own_tail = dot(jnp.concatenate(pieces, axis=0).astype(BF16), fold)
    suffix[:, :width] = sfx_latent[...]
    suffix[:, width:] = own_tail.astype(BF16)
    magnitude = jnp.maximum(
        jnp.max(jnp.abs(own_latent), axis=1, keepdims=True),
        jnp.max(jnp.abs(own_tail), axis=1, keepdims=True),
    )
    token_scale = ((magnitude + QUANT_EPS) / QUANT_TOP).astype(BF16).astype(F32)
    code = (own_latent / token_scale).astype(BF16)
    code_tail = jnp.where(iota(own_tail.shape, 1) == rope, token_scale, own_tail / token_scale)
    code_tail = code_tail.astype(BF16)

    def by_row(table):
        table = pick_column(table, column)[:, None, :]
        return jnp.broadcast_to(table, (count, 2 * block, table.shape[2])).reshape(rows, table.shape[2])

    owner_rows = by_row(owners[...])
    mine = owner_rows == own
    slot = jnp.sum(jnp.where(mine, by_row(slots[...]), 0), axis=1, keepdims=True)
    place = jnp.sum(jnp.where(mine, iota(mine.shape, 1), 0), axis=1, keepdims=True)
    row = iota((rows, 1), 0)
    unit = row % (2 * block)
    limit_shape = (rows, count)
    limit = jnp.where(
        iota(limit_shape, 1) == iota(limit_shape, 0) // (2 * block),
        jnp.broadcast_to(prefix[...], limit_shape),
        0,
    )
    limit = jnp.sum(limit, axis=1, keepdims=True)
    read = unit < block
    bias = jnp.where(read & ((place * ctx + column) * block >= limit), HIDDEN, 0.0)
    source = jnp.where(read, slot * block + unit, -1)
    take_read = (iota((rows, count * block), 1) == source).astype(F32).astype(BF16)
    mark = jnp.sum(jnp.where(iota(targets.shape, 0) == own, targets[...], 0), axis=0)
    mark = jnp.sum(jnp.where(iota(mark.shape, 0) == column, mark, 0), axis=0, keepdims=True)
    new = mark.shape[1]
    mark = jnp.broadcast_to(mark, (tokens, new))
    mark = jnp.sum(jnp.where(iota(mark.shape, 1) == iota(mark.shape, 0) // block, mark, 0), axis=1, keepdims=True)
    mark = mark * (2 * block) + block + iota((tokens, 1), 0) % block
    square = (tokens, tokens)
    mark = jnp.where(iota(square, 0) == iota(square, 1), jnp.broadcast_to(mark, square), 0)
    mark = jnp.sum(mark, axis=0, keepdims=True)
    take_new = (iota((rows, tokens), 0) == mark).astype(F32).astype(BF16)

    body = dot(take_read, keys) + dot(take_new, code)
    end = dot(take_read, key_tail) + dot(take_new, code_tail)
    end = end + jnp.where(iota(end.shape, 1) == rope, bias, 0.0)
    message[:, :, :width] = body.astype(BF16).reshape(count, 2 * block, width)
    message[:, :, width:] = end.astype(BF16).reshape(count, 2 * block, tail)


def shard_kernel(arrived, suffix, shard):
    count, double, width = arrived.shape
    block = double // 2
    shard[: count * block, :] = (
        arrived[...].astype(F32)[:, :block, :].reshape(count * block, width).astype(BF16)
    )
    shard[count * block :, :] = suffix[...]


def land_kernel(ids, arrived, targets, slots, out_latent, out_rope, out_scale):
    own, column = ids[0], ids[1]
    new, block, width = out_latent.shape
    count = arrived.shape[0]
    rope = out_rope.shape[1] // block
    tail = arrived.shape[2] - width
    target = pick_column(targets[...], column)
    slot = pick_column(slots[...], column)
    cube = (new,) + target.shape
    hit = (jnp.broadcast_to(target[None], cube) == own) & (jnp.broadcast_to(slot[None], cube) == iota(cube, 0))
    source = jnp.sum(jnp.where(hit, iota(cube, 1), 0), axis=2, keepdims=True)
    source = jnp.sum(source, axis=1, keepdims=True)
    source = jnp.broadcast_to(source, (new, block, 1)).reshape(new * block, 1)
    rows = new * block
    source = source * (2 * block) + block + iota((rows, 1), 0) % block
    take = (iota((rows, count * 2 * block), 1) == source).astype(F32).astype(BF16)
    flat = arrived[...].reshape(count * 2 * block, width + tail)
    out_latent[...] = dot(take, flat[:, :width]).astype(BF16).reshape(new, block, width)
    end = dot(take, flat[:, width:])
    fold = fold_matrix(block, rope, tail)
    wide = dot_nt(end.astype(BF16), fold)
    wide = jnp.where(iota(wide.shape, 1) // rope == iota(wide.shape, 0) % block, wide, 0.0)
    out_rope[...] = jnp.sum(wide.reshape(new, block, block * rope), axis=1).astype(BF16)
    scale = jnp.sum(jnp.where(iota(end.shape, 1) == rope, end, 0.0), axis=1, keepdims=True)
    scale = jnp.broadcast_to(scale, (rows, block))
    scale = jnp.where(iota(scale.shape, 1) == iota(scale.shape, 0) % block, scale, 0.0)
    out_scale[...] = jnp.sum(scale.reshape(new, block, block), axis=1).astype(BF16)


def absorb_kernel(nope, rotary, weight, out):
    heads, depth, width = weight.shape
    tokens = nope.shape[0]
    rope = rotary.shape[1] // heads
    tail = out.shape[2] - width
    filler = (iota((tokens, tail - rope), 1) == 0).astype(F32).astype(BF16)
    for h in range(heads):
        out[h, :, :width] = dot(nope[:, h * depth : (h + 1) * depth], weight[h]).astype(BF16)
        out[h, :, width:] = jnp.concatenate([rotary[:, h * rope : (h + 1) * rope], filler], axis=1)


def attend_kernel(shards, first, last, sub, scale, *refs):
    refs = list(refs)
    query = refs.pop(0)
    key_refs = [refs.pop(0) for _ in range(shards)]
    if not first:
        acc_in, stat_in = refs.pop(0), refs.pop(0)
    if last:
        ids, all_refs, value = refs.pop(0), refs[:8], refs[8]
        del refs[:9]
        (out,) = refs
    else:
        acc_out, stat_out = refs
    heads, tokens, wide = query.shape
    group = tokens
    prefix = key_refs[0].shape[0] - group
    width = value.shape[1] if last else acc_out.shape[2]
    step = sub // tokens
    keys = [ref[:prefix, :] for ref in key_refs]
    if last:
        suffix = jnp.concatenate([ref[prefix:, :] for ref in all_refs], axis=0)
        shape = (1, suffix.shape[0])
        where = iota(shape, 1) % group
        for i in range(len(all_refs)):
            where = where + jnp.where(iota(shape, 1) // group == i, ids[2 + i] * group, 0)
        seen = where <= ids[1] * group + iota((sub, 1), 0) % tokens
    for part in range(heads // step):
        q = query[part * step : (part + 1) * step].reshape(sub, wide)
        scores = [dot_nt(q, k) for k in keys]
        held = list(keys)
        if last:
            scores.append(jnp.where(seen, dot_nt(q, suffix), HIDDEN))
            held.append(suffix)
        tops = [jnp.max(s, axis=1, keepdims=True) for s in scores]
        if not first:
            stat = stat_in[part * step : (part + 1) * step].reshape(sub, 128)
            old_top, old_total = stat[:, 0:1], stat[:, 64:65]
            tops.append(old_top)
        top = functools.reduce(jnp.maximum, tops)
        weights = [jnp.exp((s - top) * scale) for s in scores]
        total = sum(jnp.sum(w, axis=1, keepdims=True) for w in weights)
        mixed = sum(dot(w.astype(BF16), k[:, :width]) for w, k in zip(weights, held))
        if not first:
            fade = jnp.exp((old_top - top) * scale)
            total = total + old_total * fade
            mixed = mixed + acc_in[part * step : (part + 1) * step].reshape(sub, width) * fade
        if last:
            mixed = (mixed / total).astype(BF16)
            for h in range(step):
                at = part * step + h
                out[:, at * value.shape[2] : (at + 1) * value.shape[2]] = dot(
                    mixed[h * tokens : (h + 1) * tokens], value[at]
                ).astype(BF16)
        else:
            acc_out[part * step : (part + 1) * step] = mixed.reshape(step, tokens, width)
            stat = jnp.where(iota((sub, 128), 1) < 64, top, total)
            stat_out[part * step : (part + 1) * step] = stat.reshape(step, tokens, 128)


def attend(query, shards, state=None, final=None, width=512, tile=8, sub=256, scale=1.0):
    heads, tokens, wide = query.shape
    first, last = state is None, final is not None

    def by_tile(*dims):
        return pl.BlockSpec((tile,) + dims, lambda i: (i,) + (0,) * len(dims))

    def whole(array):
        return pl.BlockSpec(array.shape, lambda i: (0,) * array.ndim)

    operands, specs = [query, *shards], [by_tile(tokens, wide)] + [whole(s) for s in shards]
    if not first:
        operands += list(state)
        specs += [by_tile(tokens, width), by_tile(tokens, 128)]
    keys = sum(s.shape[0] - tokens for s in shards)
    if last:
        ids, every, value = final
        operands += [ids, *every, value]
        specs += [SMEM] + [whole(s) for s in every] + [by_tile(*value.shape[1:])]
        lanes = value.shape[2]
        out_shape = jax.ShapeDtypeStruct((tokens, heads * lanes), BF16)
        out_specs = pl.BlockSpec((tokens, tile * lanes), lambda i: (0, i))
        keys += tokens * len(every)
    else:
        out_shape = (
            jax.ShapeDtypeStruct((heads, tokens, width), F32),
            jax.ShapeDtypeStruct((heads, tokens, 128), F32),
        )
        out_specs = (by_tile(tokens, width), by_tile(tokens, 128))
    rows = heads * tokens
    return pl.pallas_call(
        functools.partial(attend_kernel, len(shards), first, last, sub, scale),
        grid=(heads // tile,),
        in_specs=specs,
        out_specs=out_specs,
        out_shape=out_shape,
        compiler_params=pltpu.CompilerParams(vmem_limit_bytes=40 * MIB),
        cost_estimate=pl.CostEstimate(
            flops=2 * rows * keys * (wide + width), bytes_accessed=8 * MIB, transcendentals=rows * keys
        ),
    )(*operands)


def body(
    query_nope,
    query_rope,
    suffix_latent,
    suffix_rope,
    absorb_key,
    absorb_value,
    pool_latent,
    pool_rope,
    pool_scale,
    prefix_tokens,
    block_owner,
    block_slot,
    write_owner,
    write_slot,
):
    own = lax.axis_index("pool")
    column = lax.axis_index("ctx")
    count = lax.axis_size("pool")
    ctx = lax.axis_size("ctx")
    heads, nope, latent = absorb_key.shape
    tokens = query_nope.shape[1]
    rope = query_rope.shape[2] // heads
    block = pool_scale.shape[3]
    slots = pool_scale.shape[2]
    new_blocks = write_owner.shape[2]
    wide = latent + 128
    scale = (nope + rope) ** -0.5
    core = column % 2
    turn = jnp.where(core == 0, -2, 2)
    a, c = (column + turn) % ctx, (column + 2 * turn) % ctx
    a_swap = ((column ^ 1) - turn) % ctx
    c_swap = ((column ^ 1) - 2 * turn) % ctx
    order = [column, column ^ 1, a, a_swap, a ^ 1, a_swap ^ 1, c, c_swap]
    ids = jnp.stack([own, column] + order).astype(jnp.int32)

    message, suffix = pl.pallas_call(
        pack_kernel,
        in_specs=[SMEM] + [VMEM] * 9,
        out_specs=(VMEM, VMEM),
        out_shape=(
            jax.ShapeDtypeStruct((count, 2 * block, wide), BF16),
            jax.ShapeDtypeStruct((tokens, wide), BF16),
        ),
        compiler_params=pltpu.CompilerParams(vmem_limit_bytes=32 * MIB),
    )(
        ids,
        pool_latent[0, 0],
        pool_rope[0, 0],
        pool_scale[0, 0],
        suffix_latent[0],
        suffix_rope,
        prefix_tokens[None],
        block_owner,
        block_slot,
        write_owner,
    )
    arrived = lax.all_to_all(message, "pool", split_axis=0, concat_axis=0, tiled=True)

    tile = 4
    query = pl.pallas_call(
        absorb_kernel,
        grid=(heads // tile,),
        in_specs=[
            pl.BlockSpec((tokens, tile * nope), lambda i: (0, i)),
            pl.BlockSpec((tokens, tile * rope), lambda i: (0, i)),
            pl.BlockSpec((tile, nope, latent), lambda i: (i, 0, 0)),
        ],
        out_specs=pl.BlockSpec((tile, tokens, wide), lambda i: (i, 0, 0)),
        out_shape=jax.ShapeDtypeStruct((heads, tokens, wide), BF16),
        compiler_params=pltpu.CompilerParams(vmem_limit_bytes=16 * MIB),
        cost_estimate=pl.CostEstimate(
            flops=2 * heads * tokens * nope * latent, bytes_accessed=8 * MIB, transcendentals=0
        ),
    )(query_nope[0], query_rope[0], absorb_key)

    shard = pl.pallas_call(
        shard_kernel,
        in_specs=[VMEM, VMEM],
        out_specs=VMEM,
        out_shape=jax.ShapeDtypeStruct((slots * block + tokens, wide), BF16),
    )(arrived, suffix)

    ring = [(s, (s + (2 if s % 2 == 0 else -2)) % ctx) for s in range(ctx)]
    swap = [(s, s ^ 1) for s in range(ctx)]
    first = lax.ppermute(shard, "ctx", ring)
    sibling = lax.ppermute(shard, "ctx", swap)
    second = lax.ppermute(sibling, "ctx", ring)
    third = lax.ppermute(first, "ctx", ring)
    first_swap = lax.ppermute(first, "ctx", swap)
    second_swap = lax.ppermute(second, "ctx", swap)
    third_swap = lax.ppermute(third, "ctx", swap)

    run = functools.partial(attend, query, width=latent, scale=scale)
    state = run([shard, sibling])
    state = run([first, first_swap], state)
    state = run([second, second_swap], state)
    every = [shard, sibling, first, first_swap, second, second_swap, third, third_swap]
    attended = run([third, third_swap], state, (ids, every, absorb_value))

    written_latent, written_rope, written_scale = pl.pallas_call(
        land_kernel,
        in_specs=[SMEM] + [VMEM] * 3,
        out_specs=(VMEM, VMEM, VMEM),
        out_shape=(
            jax.ShapeDtypeStruct((new_blocks, block, latent), BF16),
            jax.ShapeDtypeStruct((new_blocks, block * rope), BF16),
            jax.ShapeDtypeStruct((new_blocks, block), BF16),
        ),
    )(ids, arrived, write_owner, write_slot)
    return (attended[None], written_latent[None, None], written_rope[None, None], written_scale[None, None])


def solution(mesh):
    placed = (
        P("pool", "ctx", None),
        P("pool", "ctx", None),
        P("pool", "ctx", None),
        P("pool", "ctx"),
        P(),
        P(),
        P("pool", "ctx", None, None, None),
        P("pool", "ctx", None, None),
        P("pool", "ctx", None, None),
        P(),
        P(),
        P(),
        P(),
        P(),
    )
    return jax.shard_map(
        body,
        mesh=mesh,
        in_specs=placed,
        out_specs=(
            P("pool", "ctx", None),
            P("pool", "ctx", None, None, None),
            P("pool", "ctx", None, None),
            P("pool", "ctx", None, None),
        ),
        check_vma=False,
    )
```

```python
import functools

import jax
import jax.numpy as jnp
from jax import lax
from jax.experimental import pallas as pl
from jax.experimental.pallas import tpu as pltpu
from jax.sharding import PartitionSpec as P

HIDDEN = -1e30
QUANT_TOP = 4.0
QUANT_EPS = 1e-06
MIB = 1 << 20

F32 = jnp.float32
BF16 = jnp.bfloat16
VMEM = pl.BlockSpec(memory_space=pltpu.VMEM)
SMEM = pl.BlockSpec(memory_space=pltpu.SMEM)
ANY = pl.BlockSpec(memory_space=pl.ANY)


def iota(shape, axis):
    return lax.broadcasted_iota(jnp.int32, shape, axis)


def dot(a, b):
    return jnp.dot(a, b, preferred_element_type=F32)


def dot_nt(a, b):
    return lax.dot_general(a, b, (((1,), (1,)), ((), ())), preferred_element_type=F32)


def fold_matrix(block, rope, lanes):
    shape = (block * rope, lanes)
    return (iota(shape, 0) % rope == iota(shape, 1)).astype(F32).astype(BF16)


def pick_column(table, column):
    return jnp.sum(jnp.where(iota(table.shape, 1) == column, table, 0), axis=1)


def pack_kernel(ids, latent, ropes, scales, prefix, owners, slots, message):
    own, column = ids[0], ids[1]
    count, block, width = latent.shape
    rope = ropes.shape[1] // block
    ctx = owners.shape[1]
    tail = message.shape[2] - width
    rows = block * count
    fold = fold_matrix(block, rope, tail)

    cube = (count, block, count)
    factor = jnp.broadcast_to(scales[...].astype(F32)[None], cube)
    factor = jnp.sum(jnp.where(iota(cube, 0) == iota(cube, 2), factor, 0.0), axis=2, keepdims=True)
    keys = (latent[...].astype(F32) * factor).reshape(rows, width).astype(BF16)
    wide = (count, block, block * rope)
    spread = jnp.broadcast_to(ropes[...].astype(F32)[:, None, :], wide) * factor
    spread = jnp.where(iota(wide, 2) // rope == iota(wide, 1), spread, 0.0)
    key_tail = dot(spread.reshape(rows, block * rope).astype(BF16), fold).astype(BF16)

    def by_row(table):
        table = pick_column(table, column)[:, None, :]
        return jnp.broadcast_to(table, (count, block, table.shape[2])).reshape(rows, table.shape[2])

    mine = by_row(owners[...]) == own
    slot = jnp.sum(jnp.where(mine, by_row(slots[...]), 0), axis=1, keepdims=True)
    place = jnp.sum(jnp.where(mine, iota(mine.shape, 1), 0), axis=1, keepdims=True)
    unit = iota((rows, 1), 0) % block
    limit_shape = (rows, count)
    limit = jnp.where(
        iota(limit_shape, 1) == iota(limit_shape, 0) // block,
        jnp.broadcast_to(prefix[...], limit_shape),
        0,
    )
    limit = jnp.sum(limit, axis=1, keepdims=True)
    bias = jnp.where((place * ctx + column) * block >= limit, HIDDEN, 0.0)
    take = (iota((rows, rows), 1) == slot * block + unit).astype(F32).astype(BF16)

    message[:, :, :width] = dot(take, keys).astype(BF16).reshape(count, block, width)
    end = dot(take, key_tail)
    end = end + jnp.where(iota(end.shape, 1) == rope, bias, 0.0)
    message[:, :, width:] = end.astype(BF16).reshape(count, block, tail)


def code_kernel(ids, after, sfx_latent, sfx_rope, targets, suffix, message):
    own, column = ids[0], ids[1]
    tokens, width = sfx_latent.shape
    count, block, lanes = message.shape
    rope = sfx_rope.shape[1] // tokens
    tail = lanes - width
    rows = count * block
    fold = fold_matrix(block, rope, tail)
    own_latent = sfx_latent[...].astype(F32)
    pieces = []
    for g in range(tokens // block):
        piece = sfx_rope[:, g * block * rope : (g + 1) * block * rope].astype(F32)
        piece = jnp.broadcast_to(piece, (block, block * rope))
        pieces.append(jnp.where(iota(piece.shape, 1) // rope == iota(piece.shape, 0), piece, 0.0))
    own_tail = dot(jnp.concatenate(pieces, axis=0).astype(BF16), fold)
    suffix[:, :width] = sfx_latent[...]
    suffix[:, width:] = own_tail.astype(BF16)
    magnitude = jnp.maximum(
        jnp.max(jnp.abs(own_latent), axis=1, keepdims=True),
        jnp.max(jnp.abs(own_tail), axis=1, keepdims=True),
    )
    token_scale = ((magnitude + QUANT_EPS) / QUANT_TOP).astype(BF16).astype(F32)
    code = (own_latent / token_scale).astype(BF16)
    code_tail = jnp.where(iota(own_tail.shape, 1) == rope, token_scale, own_tail / token_scale)
    code_tail = code_tail.astype(BF16)

    table = targets[...]
    mark = jnp.sum(jnp.where(iota(table.shape, 0) == column, table, 0), axis=0)
    mark = jnp.sum(jnp.where(iota(mark.shape, 1) == own, mark, 0), axis=1, keepdims=True)
    new = mark.shape[0]
    mark = jnp.broadcast_to(mark, (new, tokens))
    mark = jnp.sum(jnp.where(iota(mark.shape, 0) == iota(mark.shape, 1) // block, mark, 0), axis=0, keepdims=True)
    mark = mark * block + iota((1, tokens), 1) % block
    take = (iota((rows, tokens), 0) == mark).astype(F32).astype(BF16)
    message[:, :, :width] = dot(take, code).astype(BF16).reshape(count, block, width)
    message[:, :, width:] = dot(take, code_tail).astype(BF16).reshape(count, block, tail)


def shard_kernel(arrived, suffix, after, shard):
    rows = arrived.shape[0]
    shard[:rows, :] = arrived[...]
    shard[rows:, :] = suffix[...]


def land_kernel(ids, arrived, targets, slots, out_latent, out_rope, out_scale):
    own, column = ids[0], ids[1]
    new, block, width = out_latent.shape
    count = arrived.shape[0]
    rope = out_rope.shape[1] // block
    tail = arrived.shape[2] - width

    def pick(table):
        return jnp.sum(jnp.where(iota(table.shape, 0) == column, table, 0), axis=0)

    target, slot = pick(targets[...]), pick(slots[...])
    cube = (new,) + target.shape
    hit = (jnp.broadcast_to(target[None], cube) == own) & (jnp.broadcast_to(slot[None], cube) == iota(cube, 0))
    source = jnp.sum(jnp.where(hit, iota(cube, 2), 0), axis=2, keepdims=True)
    source = jnp.sum(source, axis=1, keepdims=True)
    rows = new * block
    source = jnp.broadcast_to(source, (new, block, 1)).reshape(rows, 1)
    source = source * block + iota((rows, 1), 0) % block
    take = (iota((rows, count * block), 1) == source).astype(F32).astype(BF16)
    flat = arrived[...].astype(F32).reshape(count * block, width + tail).astype(BF16)
    out_latent[...] = dot(take, flat[:, :width]).astype(BF16).reshape(new, block, width)
    end = dot(take, flat[:, width:])
    fold = fold_matrix(block, rope, tail)
    wide = dot_nt(end.astype(BF16), fold)
    wide = jnp.where(iota(wide.shape, 1) // rope == iota(wide.shape, 0) % block, wide, 0.0)
    out_rope[...] = jnp.sum(wide.reshape(new, block, block * rope), axis=1).astype(BF16)
    scale = jnp.sum(jnp.where(iota(end.shape, 1) == rope, end, 0.0), axis=1, keepdims=True)
    scale = jnp.broadcast_to(scale, (rows, block))
    scale = jnp.where(iota(scale.shape, 1) == iota(scale.shape, 0) % block, scale, 0.0)
    out_scale[...] = jnp.sum(scale.reshape(new, block, block), axis=1).astype(BF16)


def absorb_kernel(nope, rotary, weight, after, out):
    heads, depth, width = weight.shape
    tokens = nope.shape[0]
    rope = rotary.shape[1] // heads
    tail = out.shape[1] - width
    filler = (iota((tokens, tail - rope), 1) == 0).astype(F32).astype(BF16)
    for h in range(heads):
        rows = slice(h * tokens, (h + 1) * tokens)
        out[rows, :width] = dot(nope[:, h * depth : (h + 1) * depth], weight[h]).astype(BF16)
        out[rows, width:] = jnp.concatenate([rotary[:, h * rope : (h + 1) * rope], filler], axis=1)


LANES = 128


def attend_kernel(shards, first, last, sub, tokens, scale, *refs):
    refs = list(refs)
    query = refs.pop(0)
    key_refs = [refs.pop(0) for _ in range(shards)]
    if not first:
        acc_in, top_in, total_in = refs.pop(0), refs.pop(0), refs.pop(0)
    if last:
        ids, all_refs, value = refs.pop(0), refs[:8], refs[8]
        del refs[:9]
        (out,) = refs
    else:
        acc_out, top_out, total_out = refs
    prefix = key_refs[0].shape[0] - tokens
    width = value.shape[1] if last else acc_out.shape[1]
    keys = [ref[:prefix, :] for ref in key_refs]
    if last:
        suffix = jnp.concatenate([ref[prefix:, :] for ref in all_refs], axis=0)
        shape = (1, suffix.shape[0])
        place = iota(shape, 1) % tokens
        for i in range(len(all_refs)):
            place = place + jnp.where(iota(shape, 1) // tokens == i, ids[2 + i] * tokens, 0)
        seen = place <= ids[1] * tokens + iota((sub, 1), 0) % tokens
    for part in range(query.shape[0] // sub):
        rows = slice(part * sub, (part + 1) * sub)
        q = query[rows, :]
        scores = [dot_nt(q, k) for k in keys]
        held = list(keys)
        if last:
            scores.append(jnp.where(seen, dot_nt(q, suffix), HIDDEN))
            held.append(suffix)
        top = functools.reduce(jnp.maximum, [jnp.max(s, axis=1, keepdims=True) for s in scores])
        weights = [jnp.exp((s - top) * scale) for s in scores]
        total = sum(jnp.sum(w, axis=1, keepdims=True) for w in weights)
        mixed = sum(dot(w.astype(BF16), k[:, :width]) for w, k in zip(weights, held))
        top = jnp.broadcast_to(top, (sub, LANES))
        total = jnp.broadcast_to(total, (sub, LANES))
        if first:
            acc_out[rows, :] = mixed
            top_out[rows, :] = top
            total_out[rows, :] = total
            continue
        joint = jnp.maximum(top, top_in[rows, :])
        gain = jnp.exp((top - joint) * scale)
        fade = jnp.exp((top_in[rows, :] - joint) * scale)
        total = total * gain + total_in[rows, :] * fade
        if last:
            inverse = 1.0 / total
            gain, fade = gain * inverse, fade * inverse
        chunks = []
        for c in range(width // LANES):
            at = slice(c * LANES, (c + 1) * LANES)
            chunk = mixed[:, at] * gain + acc_in[rows, at] * fade
            if last:
                chunks.append(chunk.astype(BF16))
            else:
                acc_out[rows, at] = chunk
        if last:
            mixed = jnp.concatenate(chunks, axis=1)
            lanes = value.shape[2]
            for h in range(sub // tokens):
                head = part * (sub // tokens) + h
                out[:, head * lanes : (head + 1) * lanes] = dot(
                    mixed[h * tokens : (h + 1) * tokens], value[head]
                ).astype(BF16)
        else:
            top_out[rows, :] = joint
            total_out[rows, :] = total


def attend(query, shards, tokens, width, scale, state=None, final=None, sub=1024):
    rows, wide = query.shape
    first, last = state is None, final is not None
    operands, specs = [query, *shards], [VMEM] * (1 + len(shards))
    if not first:
        operands += list(state)
        specs += [VMEM] * 3
    keys = sum(s.shape[0] - tokens for s in shards)
    if last:
        ids, every, value = final
        operands += [ids, *every, value]
        specs += [SMEM] + [VMEM] * (len(every) + 1)
        out_shape = jax.ShapeDtypeStruct((tokens, rows // tokens * value.shape[2]), BF16)
        out_specs = VMEM
        keys += tokens * len(every)
    else:
        out_shape = tuple(jax.ShapeDtypeStruct((rows, n), F32) for n in (width, LANES, LANES))
        out_specs = (VMEM, VMEM, VMEM)
    return pl.pallas_call(
        functools.partial(attend_kernel, len(shards), first, last, sub, tokens, scale),
        in_specs=specs,
        out_specs=out_specs,
        out_shape=out_shape,
        compiler_params=pltpu.CompilerParams(vmem_limit_bytes=24 * MIB),
        cost_estimate=pl.CostEstimate(
            flops=2 * rows * keys * (wide + width), bytes_accessed=MIB, transcendentals=rows * keys
        ),
    )(*operands)


def body(
    query_nope,
    query_rope,
    suffix_latent,
    suffix_rope,
    absorb_key,
    absorb_value,
    pool_latent,
    pool_rope,
    pool_scale,
    prefix_tokens,
    block_owner,
    block_slot,
    write_owner,
    write_slot,
):
    own = lax.axis_index("pool")
    column = lax.axis_index("ctx")
    count = lax.axis_size("pool")
    ctx = lax.axis_size("ctx")
    heads, nope, latent = absorb_key.shape
    tokens = query_nope.shape[1]
    rope = query_rope.shape[2] // heads
    block = pool_scale.shape[3]
    slots = pool_scale.shape[2]
    new_blocks = write_owner.shape[2]
    wide = latent + 128
    scale = (nope + rope) ** -0.5
    core = column % 2
    turn = jnp.where(core == 0, -2, 2)
    a, c = (column + turn) % ctx, (column + 2 * turn) % ctx
    a_swap = ((column ^ 1) - turn) % ctx
    c_swap = ((column ^ 1) - 2 * turn) % ctx
    order = [column, column ^ 1, a, a_swap, a ^ 1, a_swap ^ 1, c, c_swap]
    ids = jnp.stack([own, column] + order).astype(jnp.int32)

    rows = slots * block
    message = pl.pallas_call(
        pack_kernel,
        in_specs=[SMEM] + [VMEM] * 6,
        out_specs=VMEM,
        out_shape=jax.ShapeDtypeStruct((count, block, wide), BF16),
        compiler_params=pltpu.CompilerParams(vmem_limit_bytes=60 * MIB),
    )(ids, pool_latent[0, 0], pool_rope[0, 0], pool_scale[0, 0].T, prefix_tokens[None], block_owner, block_slot)
    arrived = lax.all_to_all(message, "pool", split_axis=0, concat_axis=0, tiled=True)

    targets, target_slots = jnp.transpose(write_owner, (1, 2, 0)), jnp.transpose(write_slot, (1, 2, 0))
    suffix, codes = pl.pallas_call(
        code_kernel,
        in_specs=[SMEM, ANY] + [VMEM] * 3,
        out_specs=(VMEM, VMEM),
        out_shape=(
            jax.ShapeDtypeStruct((tokens, wide), BF16),
            jax.ShapeDtypeStruct((count, block, wide), BF16),
        ),
        compiler_params=pltpu.CompilerParams(vmem_limit_bytes=4 * MIB),
        cost_estimate=pl.CostEstimate(flops=10**8, bytes_accessed=MIB, transcendentals=0),
    )(ids, message, suffix_latent[0], suffix_rope, targets)
    landed = lax.all_to_all(codes, "pool", split_axis=0, concat_axis=0, tiled=True)

    tile = 4
    query = pl.pallas_call(
        absorb_kernel,
        grid=(heads // tile,),
        in_specs=[
            pl.BlockSpec((tokens, tile * nope), lambda i: (0, i)),
            pl.BlockSpec((tokens, tile * rope), lambda i: (0, i)),
            pl.BlockSpec((tile, nope, latent), lambda i: (i, 0, 0)),
            ANY,
        ],
        out_specs=pl.BlockSpec((tile * tokens, wide), lambda i: (i, 0)),
        out_shape=jax.ShapeDtypeStruct((heads * tokens, wide), BF16),
        compiler_params=pltpu.CompilerParams(vmem_limit_bytes=8 * MIB),
        cost_estimate=pl.CostEstimate(
            flops=2 * heads * tokens * nope * latent, bytes_accessed=8 * MIB, transcendentals=0
        ),
    )(query_nope[0], query_rope[0], absorb_key, codes)

    shard = pl.pallas_call(
        shard_kernel,
        in_specs=[VMEM, VMEM, ANY],
        out_specs=VMEM,
        out_shape=jax.ShapeDtypeStruct((rows + tokens, wide), BF16),
        compiler_params=pltpu.CompilerParams(vmem_limit_bytes=4 * MIB),
    )(arrived.reshape(rows, wide), suffix, query)

    ring = [(s, (s + (2 if s % 2 == 0 else -2)) % ctx) for s in range(ctx)]
    swap = [(s, s ^ 1) for s in range(ctx)]
    first = lax.ppermute(shard, "ctx", ring)
    sibling = lax.ppermute(shard, "ctx", swap)
    second = lax.ppermute(sibling, "ctx", ring)
    third = lax.ppermute(first, "ctx", ring)
    first_swap = lax.ppermute(first, "ctx", swap)
    second_swap = lax.ppermute(second, "ctx", swap)
    third_swap = lax.ppermute(third, "ctx", swap)

    run = functools.partial(attend, query, tokens=tokens, width=latent, scale=scale)
    state = run([shard, sibling])
    state = run([first, first_swap], state=state)
    state = run([second, second_swap], state=state)
    every = [shard, sibling, first, first_swap, second, second_swap, third, third_swap]
    attended = run([third, third_swap], state=state, final=(ids, every, absorb_value))

    written_latent, written_rope, written_scale = pl.pallas_call(
        land_kernel,
        in_specs=[SMEM] + [VMEM] * 3,
        out_specs=(VMEM, VMEM, VMEM),
        out_shape=(
            jax.ShapeDtypeStruct((new_blocks, block, latent), BF16),
            jax.ShapeDtypeStruct((new_blocks, block * rope), BF16),
            jax.ShapeDtypeStruct((new_blocks, block), BF16),
        ),
        compiler_params=pltpu.CompilerParams(vmem_limit_bytes=8 * MIB),
    )(ids, landed, targets, target_slots)
    return (attended[None], written_latent[None, None], written_rope[None, None], written_scale[None, None])


def solution(mesh):
    placed = (
        P("pool", "ctx", None),
        P("pool", "ctx", None),
        P("pool", "ctx", None),
        P("pool", "ctx"),
        P(),
        P(),
        P("pool", "ctx", None, None, None),
        P("pool", "ctx", None, None),
        P("pool", "ctx", None, None),
        P(),
        P(),
        P(),
        P(),
        P(),
    )
    return jax.shard_map(
        body,
        mesh=mesh,
        in_specs=placed,
        out_specs=(
            P("pool", "ctx", None),
            P("pool", "ctx", None, None, None),
            P("pool", "ctx", None, None),
            P("pool", "ctx", None, None),
        ),
        check_vma=False,
    )
```

```python
import functools

import jax
import jax.numpy as jnp
from jax import lax
from jax.experimental import pallas as pl
from jax.experimental.pallas import tpu as pltpu
from jax.sharding import PartitionSpec as P

HIDDEN = -1e30
QUANT_TOP = 4.0
QUANT_EPS = 1e-06
MIB = 1 << 20
LANES = 128

F32 = jnp.float32
BF16 = jnp.bfloat16
VMEM = pl.BlockSpec(memory_space=pltpu.VMEM)
SMEM = pl.BlockSpec(memory_space=pltpu.SMEM)
ANY = pl.BlockSpec(memory_space=pl.ANY)
HBM = pl.BlockSpec(memory_space=pltpu.HBM)


def iota(shape, axis):
    return lax.broadcasted_iota(jnp.int32, shape, axis)


def dot(a, b):
    return jnp.dot(a, b, preferred_element_type=F32)


def dot_nt(a, b):
    return lax.dot_general(a, b, (((1,), (1,)), ((), ())), preferred_element_type=F32)


def fold_matrix(block, rope, lanes):
    shape = (block * rope, lanes)
    return (iota(shape, 0) % rope == iota(shape, 1)).astype(F32).astype(BF16)


def pick_column(table, column):
    return jnp.sum(jnp.where(iota(table.shape, 1) == column, table, 0), axis=1)


def fetch(sources, held, semaphores):
    copies = [
        pltpu.make_async_copy(source, target, semaphores.at[i])
        for i, (source, target) in enumerate(zip(sources, held))
    ]
    for copy in copies:
        copy.start()
    return copies


def pack_kernel(own_ref, column_ref, *refs):
    message, suffix, semaphores = refs[9], refs[10], refs[20]
    for copy in fetch(refs[:9], refs[11:20], semaphores):
        copy.wait()
    latent, ropes, scales, sfx_latent, sfx_rope, prefix, owners, slots, targets = refs[11:20]
    own, column = own_ref[0], column_ref[0]
    count, block, width = latent.shape
    rope = ropes.shape[1] // block
    ctx = owners.shape[1]
    tokens = sfx_latent.shape[0]
    tail = message.shape[2] - width
    rows = 2 * block * count
    fold = fold_matrix(block, rope, tail)

    cube = (count, block, count)
    factor = jnp.broadcast_to(scales[...].astype(F32)[None], cube)
    factor = jnp.sum(jnp.where(iota(cube, 0) == iota(cube, 2), factor, 0.0), axis=2, keepdims=True)
    keys = (latent[...].astype(F32) * factor).reshape(count * block, width).astype(BF16)
    wide = (count, block, block * rope)
    spread = jnp.broadcast_to(ropes[...].astype(F32)[:, None, :], wide) * factor
    spread = jnp.where(iota(wide, 2) // rope == iota(wide, 1), spread, 0.0)
    key_tail = dot(spread.reshape(count * block, block * rope).astype(BF16), fold).astype(BF16)

    own_latent = sfx_latent[...].astype(F32)
    pieces = []
    for g in range(tokens // block):
        piece = sfx_rope[:, g * block * rope : (g + 1) * block * rope].astype(F32)
        piece = jnp.broadcast_to(piece, (block, block * rope))
        pieces.append(jnp.where(iota(piece.shape, 1) // rope == iota(piece.shape, 0), piece, 0.0))
    own_tail = dot(jnp.concatenate(pieces, axis=0).astype(BF16), fold)
    suffix[:, :width] = sfx_latent[...]
    suffix[:, width:] = own_tail.astype(BF16)
    magnitude = jnp.maximum(
        jnp.max(jnp.abs(own_latent), axis=1, keepdims=True),
        jnp.max(jnp.abs(own_tail), axis=1, keepdims=True),
    )
    token_scale = ((magnitude + QUANT_EPS) / QUANT_TOP).astype(BF16).astype(F32)
    code = (own_latent / token_scale).astype(BF16)
    code_tail = jnp.where(iota(own_tail.shape, 1) == rope, token_scale, own_tail / token_scale)
    code_tail = code_tail.astype(BF16)

    def by_row(table):
        table = pick_column(table, column)[:, None, :]
        return jnp.broadcast_to(table, (count, 2 * block, table.shape[2])).reshape(rows, table.shape[2])

    mine = by_row(owners[...]) == own
    slot = jnp.sum(jnp.where(mine, by_row(slots[...]), 0), axis=1, keepdims=True)
    place = jnp.sum(jnp.where(mine, iota(mine.shape, 1), 0), axis=1, keepdims=True)
    unit = iota((rows, 1), 0) % (2 * block)
    limit_shape = (rows, count)
    limit = jnp.where(
        iota(limit_shape, 1) == iota(limit_shape, 0) // (2 * block),
        jnp.broadcast_to(prefix[...], limit_shape),
        0,
    )
    limit = jnp.sum(limit, axis=1, keepdims=True)
    read = unit < block
    bias = jnp.where(read & ((place * ctx + column) * block >= limit), HIDDEN, 0.0)
    source = jnp.where(read, slot * block + unit, -1)
    take_read = (iota((rows, count * block), 1) == source).astype(F32).astype(BF16)
    table = targets[...]
    mark = jnp.sum(jnp.where(iota(table.shape, 0) == column, table, 0), axis=0)
    mark = jnp.sum(jnp.where(iota(mark.shape, 1) == own, mark, 0), axis=1, keepdims=True)
    new = mark.shape[0]
    mark = jnp.broadcast_to(mark, (new, tokens))
    mark = jnp.sum(jnp.where(iota(mark.shape, 0) == iota(mark.shape, 1) // block, mark, 0), axis=0, keepdims=True)
    mark = mark * (2 * block) + block + iota((1, tokens), 1) % block
    take_new = (iota((rows, tokens), 0) == mark).astype(F32).astype(BF16)

    body = dot(take_read, keys) + dot(take_new, code)
    end = dot(take_read, key_tail) + dot(take_new, code_tail)
    end = end + jnp.where(iota(end.shape, 1) == rope, bias, 0.0)
    message[:, :, :width] = body.astype(BF16).reshape(count, 2 * block, width)
    message[:, :, width:] = end.astype(BF16).reshape(count, 2 * block, tail)


def shard_kernel(arrived, after_group, after_query, shard):
    count, double, width = arrived.shape
    block = double // 2
    shard[...] = arrived[...].astype(F32)[:, :block, :].reshape(count * block, width).astype(BF16)


def join_kernel(*refs):
    *pieces, out, done = refs
    rows = pieces[0].shape[0]
    for i, piece in enumerate(pieces):
        out[i * rows : (i + 1) * rows, :] = piece[...]
    done[...] = jnp.zeros_like(done)


def join(*pieces):
    rows, wide = pieces[0].shape
    return pl.pallas_call(
        join_kernel,
        in_specs=[VMEM] * len(pieces),
        out_specs=(VMEM, VMEM),
        out_shape=(
            jax.ShapeDtypeStruct((rows * len(pieces), wide), BF16),
            jax.ShapeDtypeStruct((8, LANES), F32),
        ),
        compiler_params=pltpu.CompilerParams(vmem_limit_bytes=2 * MIB),
    )(*pieces)


def land_kernel(own_ref, column_ref, arrived, targets, slots, out_latent, out_rope, out_scale, done):
    done[...] = jnp.zeros_like(done)
    own, column = own_ref[0], column_ref[0]
    new, block, width = out_latent.shape
    count, double, _ = arrived.shape
    rope = out_rope.shape[1] // block
    tail = arrived.shape[2] - width

    def pick(table):
        return jnp.sum(jnp.where(iota(table.shape, 0) == column, table, 0), axis=0)

    target, slot = pick(targets[...]), pick(slots[...])
    cube = (new,) + target.shape
    hit = (jnp.broadcast_to(target[None], cube) == own) & (jnp.broadcast_to(slot[None], cube) == iota(cube, 0))
    source = jnp.sum(jnp.where(hit, iota(cube, 2), 0), axis=2, keepdims=True)
    source = jnp.sum(source, axis=1, keepdims=True)
    rows = new * block
    source = jnp.broadcast_to(source, (new, block, 1)).reshape(rows, 1)
    source = source * double + block + iota((rows, 1), 0) % block
    take = (iota((rows, count * double), 1) == source).astype(F32).astype(BF16)
    flat = arrived[...].reshape(count * double, width + tail)
    out_latent[...] = dot(take, flat[:, :width]).astype(BF16).reshape(new, block, width)
    end = dot(take, flat[:, width:])
    fold = fold_matrix(block, rope, tail)
    wide = dot_nt(end.astype(BF16), fold)
    wide = jnp.where(iota(wide.shape, 1) // rope == iota(wide.shape, 0) % block, wide, 0.0)
    out_rope[...] = jnp.sum(wide.reshape(new, block, block * rope), axis=1).astype(BF16)
    scale = jnp.sum(jnp.where(iota(end.shape, 1) == rope, end, 0.0), axis=1, keepdims=True)
    scale = jnp.broadcast_to(scale, (rows, block))
    scale = jnp.where(iota(scale.shape, 1) == iota(scale.shape, 0) % block, scale, 0.0)
    out_scale[...] = jnp.sum(scale.reshape(new, block, block), axis=1).astype(BF16)


def absorb_kernel(nope_hbm, rotary_hbm, weight_hbm, after, out, done, nope, rotary, weight, semaphores):
    done[...] = jnp.zeros_like(done)
    heads, depth, width = weight.shape
    tokens = nope.shape[0]
    rope = rotary.shape[1] // heads
    tail = out.shape[1] - width
    chunk = 8
    parts = [pl.ds(i * chunk, chunk) for i in range(heads // chunk)]
    copies = fetch(
        [nope_hbm, rotary_hbm] + [weight_hbm.at[p] for p in parts],
        [nope, rotary] + [weight.at[p] for p in parts],
        semaphores,
    )
    copies[0].wait()
    copies[1].wait()
    filler = (iota((tokens, tail - rope), 1) == 0).astype(F32).astype(BF16)
    for h in range(heads):
        if h % chunk == 0:
            copies[2 + h // chunk].wait()
        rows = slice(h * tokens, (h + 1) * tokens)
        out[rows, :width] = dot(nope[:, h * depth : (h + 1) * depth], weight[h]).astype(BF16)
        out[rows, width:] = jnp.concatenate([rotary[:, h * rope : (h + 1) * rope], filler], axis=1)


def attend_kernel(groups, blocks, first, last, sub, tokens, scale, *refs):
    refs = list(refs)
    query = refs.pop(0)
    if groups:
        group_ref = refs.pop(0)
    block_refs = [refs.pop(0) for _ in range(blocks)]
    if groups:
        column = refs.pop(0)[0]
    if not first:
        acc_in, top_in, total_in = refs.pop(0), refs.pop(0), refs.pop(0)
    if last:
        value, out = refs
    else:
        acc_out, top_out, total_out = refs
    width = value.shape[1] if last else acc_out.shape[1]
    keys = [ref[...] for ref in block_refs]
    if groups:
        keys.insert(0, group_ref[...])
        ctx = group_ref.shape[0] // tokens
        core = lax.rem(column, 2)
        turn = 4 * core - 2
        order = [column, column + turn, column + 1 - 2 * core - turn, column + 2 * turn]
        order = [lax.rem(index + ctx, ctx) for index in order]
        order = [c for index in order for c in (index, index + 1 - 2 * core)]
        shape = (1, keys[0].shape[0])
        place = iota(shape, 1) % tokens
        for i, index in enumerate(order):
            place = place + jnp.where(iota(shape, 1) // tokens == i, index * tokens, 0)
        seen = place <= column * tokens + iota((sub, 1), 0) % tokens
    for part in range(query.shape[0] // sub):
        rows = slice(part * sub, (part + 1) * sub)
        q = query[rows, :]
        scores = [dot_nt(q, k) for k in keys]
        if groups:
            scores[0] = jnp.where(seen, scores[0], HIDDEN)
        top = functools.reduce(jnp.maximum, [jnp.max(s, axis=1, keepdims=True) for s in scores])
        weights = [jnp.exp((s - top) * scale) for s in scores]
        total = sum(jnp.sum(w, axis=1, keepdims=True) for w in weights)
        mixed = sum(dot(w.astype(BF16), k[:, :width]) for w, k in zip(weights, keys))
        top = jnp.broadcast_to(top, (sub, LANES))
        total = jnp.broadcast_to(total, (sub, LANES))
        if first:
            acc_out[rows, :] = mixed
            top_out[rows, :] = top
            total_out[rows, :] = total
            continue
        joint = jnp.maximum(top, top_in[rows, :])
        gain = jnp.exp((top - joint) * scale)
        fade = jnp.exp((top_in[rows, :] - joint) * scale)
        total = total * gain + total_in[rows, :] * fade
        if last:
            inverse = 1.0 / total
            gain, fade = gain * inverse, fade * inverse
        chunks = []
        for c in range(width // LANES):
            at = slice(c * LANES, (c + 1) * LANES)
            chunk = mixed[:, at] * gain + acc_in[rows, at] * fade
            if last:
                chunks.append(chunk.astype(BF16))
            else:
                acc_out[rows, at] = chunk
        if last:
            mixed = jnp.concatenate(chunks, axis=1)
            lanes = value.shape[2]
            for h in range(sub // tokens):
                head = part * (sub // tokens) + h
                out[:, head * lanes : (head + 1) * lanes] = dot(
                    mixed[h * tokens : (h + 1) * tokens], value[head]
                ).astype(BF16)
        else:
            top_out[rows, :] = joint
            total_out[rows, :] = total


def attend(query, blocks, tokens, width, scale, group=None, column=None, state=None, value=None, sub=1024):
    rows, wide = query.shape
    first, last = state is None, value is not None
    groups = group is not None
    operands = [query] + [group] * groups + list(blocks)
    specs = [VMEM] * len(operands)
    keys = sum(k.shape[0] for k in operands[1:])
    if groups:
        operands.append(column)
        specs.append(SMEM)
    if not first:
        operands += list(state)
        specs += [VMEM] * 3
    if last:
        operands.append(value)
        specs.append(VMEM)
        out_shape = jax.ShapeDtypeStruct((tokens, rows // tokens * value.shape[2]), BF16)
        out_specs = VMEM
    else:
        out_shape = tuple(jax.ShapeDtypeStruct((rows, n), F32) for n in (width, LANES, LANES))
        out_specs = (VMEM, VMEM, VMEM)
    return pl.pallas_call(
        functools.partial(attend_kernel, groups, len(blocks), first, last, sub, tokens, scale),
        in_specs=specs,
        out_specs=out_specs,
        out_shape=out_shape,
        compiler_params=pltpu.CompilerParams(vmem_limit_bytes=24 * MIB),
        cost_estimate=pl.CostEstimate(
            flops=2 * rows * keys * (wide + width), bytes_accessed=MIB, transcendentals=rows * keys
        ),
    )(*operands)


def body(
    query_nope,
    query_rope,
    suffix_latent,
    suffix_rope,
    absorb_key,
    absorb_value,
    pool_latent,
    pool_rope,
    pool_scale,
    prefix_tokens,
    block_owner,
    block_slot,
    write_owner,
    write_slot,
):
    own = lax.axis_index("pool")
    column = lax.axis_index("ctx")
    count = lax.axis_size("pool")
    ctx = lax.axis_size("ctx")
    heads, nope, latent = absorb_key.shape
    tokens = query_nope.shape[1]
    rope = query_rope.shape[2] // heads
    block = pool_scale.shape[3]
    slots = pool_scale.shape[2]
    new_blocks = write_owner.shape[2]
    wide = latent + 128
    scale = (nope + rope) ** -0.5
    own_at, column_at = own.reshape(1), column.reshape(1)
    ring = [(s, (s + (2 if s % 2 == 0 else -2)) % ctx) for s in range(ctx)]
    swap = [(s, s ^ 1) for s in range(ctx)]

    rows = slots * block
    targets, target_slots = jnp.transpose(write_owner, (1, 2, 0)), jnp.transpose(write_slot, (1, 2, 0))
    operands = (
        pool_latent[0, 0],
        pool_rope[0, 0],
        pool_scale[0, 0].T,
        suffix_latent[0],
        suffix_rope,
        prefix_tokens[None],
        block_owner,
        block_slot,
        targets,
    )
    message, suffix = pl.pallas_call(
        pack_kernel,
        in_specs=[SMEM, SMEM] + [HBM] * len(operands),
        out_specs=(VMEM, VMEM),
        out_shape=(
            jax.ShapeDtypeStruct((count, 2 * block, wide), BF16),
            jax.ShapeDtypeStruct((tokens, wide), BF16),
        ),
        scratch_shapes=[pltpu.VMEM(x.shape, x.dtype) for x in operands]
        + [pltpu.SemaphoreType.DMA((len(operands),))],
        compiler_params=pltpu.CompilerParams(vmem_limit_bytes=60 * MIB),
    )(own_at, column_at, *operands)
    arrived = lax.all_to_all(message, "pool", split_axis=0, concat_axis=0, tiled=True)

    pair, _ = join(suffix, lax.ppermute(suffix, "ctx", swap))
    pair_first = lax.ppermute(pair, "ctx", ring)
    operands = (query_nope[0], query_rope[0], absorb_key)
    query, query_done = pl.pallas_call(
        absorb_kernel,
        in_specs=[HBM] * 3 + [ANY],
        out_specs=(VMEM, VMEM),
        out_shape=(jax.ShapeDtypeStruct((heads * tokens, wide), BF16), jax.ShapeDtypeStruct((8, LANES), F32)),
        scratch_shapes=[pltpu.VMEM(x.shape, x.dtype) for x in operands]
        + [pltpu.SemaphoreType.DMA((2 + heads // 8,))],
        compiler_params=pltpu.CompilerParams(vmem_limit_bytes=16 * MIB),
        cost_estimate=pl.CostEstimate(
            flops=2 * heads * tokens * nope * latent, bytes_accessed=8 * MIB, transcendentals=0
        ),
    )(*operands, pair)

    pair_swap = lax.ppermute(pair_first, "ctx", swap)
    pair_far = lax.ppermute(pair_first, "ctx", ring)
    group, group_done = join(pair, pair_first, pair_swap, pair_far)

    shard = pl.pallas_call(
        shard_kernel,
        in_specs=[VMEM, ANY, ANY],
        out_specs=VMEM,
        out_shape=jax.ShapeDtypeStruct((rows, wide), BF16),
        compiler_params=pltpu.CompilerParams(vmem_limit_bytes=4 * MIB),
    )(arrived, group_done, query_done)

    run = functools.partial(attend, query, tokens=tokens, width=latent, scale=scale)
    first = lax.ppermute(shard, "ctx", ring)
    sibling = lax.ppermute(shard, "ctx", swap)
    state = run([], group=group, column=column_at)
    sibling, first, total = lax.optimization_barrier((sibling, first, state[2]))
    second = lax.ppermute(sibling, "ctx", ring)
    first_swap = lax.ppermute(first, "ctx", swap)
    third = lax.ppermute(first, "ctx", ring)
    state = run([shard, sibling], state=(state[0], state[1], total))
    written_latent, written_rope, written_scale, landed = pl.pallas_call(
        land_kernel,
        in_specs=[SMEM, SMEM] + [VMEM] * 3,
        out_specs=(VMEM,) * 4,
        out_shape=(
            jax.ShapeDtypeStruct((new_blocks, block, latent), BF16),
            jax.ShapeDtypeStruct((new_blocks, block * rope), BF16),
            jax.ShapeDtypeStruct((new_blocks, block), BF16),
            jax.ShapeDtypeStruct((8, LANES), F32),
        ),
        compiler_params=pltpu.CompilerParams(vmem_limit_bytes=8 * MIB),
    )(own_at, column_at, arrived, targets, target_slots)
    first_swap, landed = lax.optimization_barrier((first_swap, landed))
    state = run([first, first_swap], state=state)
    second, third, total = lax.optimization_barrier((second, third, state[2]))
    second_swap = lax.ppermute(second, "ctx", swap)
    third_swap = lax.ppermute(third, "ctx", swap)
    state = run([second, third], state=(state[0], state[1], total))
    attended = run([second_swap, third_swap], state=state, value=absorb_value)
    return (attended[None], written_latent[None, None], written_rope[None, None], written_scale[None, None])


def solution(mesh):
    placed = (
        P("pool", "ctx", None),
        P("pool", "ctx", None),
        P("pool", "ctx", None),
        P("pool", "ctx"),
        P(),
        P(),
        P("pool", "ctx", None, None, None),
        P("pool", "ctx", None, None),
        P("pool", "ctx", None, None),
        P(),
        P(),
        P(),
        P(),
        P(),
    )
    return jax.shard_map(
        body,
        mesh=mesh,
        in_specs=placed,
        out_specs=(
            P("pool", "ctx", None),
            P("pool", "ctx", None, None, None),
            P("pool", "ctx", None, None),
            P("pool", "ctx", None, None),
        ),
        check_vma=False,
    )
```

```python
import functools

import jax
import jax.numpy as jnp
from jax import lax
from jax.experimental import pallas as pl
from jax.experimental.pallas import tpu as pltpu
from jax.sharding import PartitionSpec as P

HIDDEN = -1e30
QUANT_TOP = 4.0
QUANT_EPS = 1e-06
MIB = 1 << 20
LANES = 128

F32 = jnp.float32
BF16 = jnp.bfloat16
VMEM = pl.BlockSpec(memory_space=pltpu.VMEM)
SMEM = pl.BlockSpec(memory_space=pltpu.SMEM)
ANY = pl.BlockSpec(memory_space=pl.ANY)
HBM = pl.BlockSpec(memory_space=pltpu.HBM)


def iota(shape, axis):
    return lax.broadcasted_iota(jnp.int32, shape, axis)


def dot(a, b):
    return jnp.dot(a, b, preferred_element_type=F32)


def dot_nt(a, b):
    return lax.dot_general(a, b, (((1,), (1,)), ((), ())), preferred_element_type=F32)


def fold_matrix(block, rope, lanes):
    shape = (block * rope, lanes)
    return (iota(shape, 0) % rope == iota(shape, 1)).astype(F32).astype(BF16)


def pick_column(table, column):
    return jnp.sum(jnp.where(iota(table.shape, 1) == column, table, 0), axis=1)


def fetch(sources, held, semaphores):
    copies = [
        pltpu.make_async_copy(source, target, semaphores.at[i])
        for i, (source, target) in enumerate(zip(sources, held))
    ]
    for copy in copies:
        copy.start()
    return copies


def pack_kernel(own_ref, column_ref, *refs):
    message, suffix, semaphores = refs[9], refs[10], refs[20]
    for copy in fetch(refs[:9], refs[11:20], semaphores):
        copy.wait()
    latent, ropes, scales, sfx_latent, sfx_rope, prefix, owners, slots, targets = refs[11:20]
    own, column = own_ref[0], column_ref[0]
    count, block, width = latent.shape
    rope = ropes.shape[1] // block
    ctx = owners.shape[1]
    tokens = sfx_latent.shape[0]
    tail = message.shape[2] - width
    rows = 2 * block * count
    fold = fold_matrix(block, rope, tail)

    cube = (count, block, count)
    factor = jnp.broadcast_to(scales[...].astype(F32)[None], cube)
    factor = jnp.sum(jnp.where(iota(cube, 0) == iota(cube, 2), factor, 0.0), axis=2, keepdims=True)
    keys = (latent[...].astype(F32) * factor).reshape(count * block, width).astype(BF16)
    wide = (count, block, block * rope)
    spread = jnp.broadcast_to(ropes[...].astype(F32)[:, None, :], wide) * factor
    spread = jnp.where(iota(wide, 2) // rope == iota(wide, 1), spread, 0.0)
    key_tail = dot(spread.reshape(count * block, block * rope).astype(BF16), fold).astype(BF16)

    own_latent = sfx_latent[...].astype(F32)
    pieces = []
    for g in range(tokens // block):
        piece = sfx_rope[:, g * block * rope : (g + 1) * block * rope].astype(F32)
        piece = jnp.broadcast_to(piece, (block, block * rope))
        pieces.append(jnp.where(iota(piece.shape, 1) // rope == iota(piece.shape, 0), piece, 0.0))
    own_tail = dot(jnp.concatenate(pieces, axis=0).astype(BF16), fold)
    suffix[:, :width] = sfx_latent[...]
    suffix[:, width:] = own_tail.astype(BF16)
    magnitude = jnp.maximum(
        jnp.max(jnp.abs(own_latent), axis=1, keepdims=True),
        jnp.max(jnp.abs(own_tail), axis=1, keepdims=True),
    )
    token_scale = ((magnitude + QUANT_EPS) / QUANT_TOP).astype(BF16).astype(F32)
    code = (own_latent / token_scale).astype(BF16)
    code_tail = jnp.where(iota(own_tail.shape, 1) == rope, token_scale, own_tail / token_scale)
    code_tail = code_tail.astype(BF16)

    def by_row(table):
        table = pick_column(table, column)[:, None, :]
        return jnp.broadcast_to(table, (count, 2 * block, table.shape[2])).reshape(rows, table.shape[2])

    mine = by_row(owners[...]) == own
    slot = jnp.sum(jnp.where(mine, by_row(slots[...]), 0), axis=1, keepdims=True)
    place = jnp.sum(jnp.where(mine, iota(mine.shape, 1), 0), axis=1, keepdims=True)
    unit = iota((rows, 1), 0) % (2 * block)
    limit_shape = (rows, count)
    limit = jnp.where(
        iota(limit_shape, 1) == iota(limit_shape, 0) // (2 * block),
        jnp.broadcast_to(prefix[...], limit_shape),
        0,
    )
    limit = jnp.sum(limit, axis=1, keepdims=True)
    read = unit < block
    bias = jnp.where(read & ((place * ctx + column) * block >= limit), HIDDEN, 0.0)
    source = jnp.where(read, slot * block + unit, -1)
    take_read = (iota((rows, count * block), 1) == source).astype(F32).astype(BF16)
    table = targets[...]
    mark = jnp.sum(jnp.where(iota(table.shape, 0) == column, table, 0), axis=0)
    mark = jnp.sum(jnp.where(iota(mark.shape, 1) == own, mark, 0), axis=1, keepdims=True)
    new = mark.shape[0]
    mark = jnp.broadcast_to(mark, (new, tokens))
    mark = jnp.sum(jnp.where(iota(mark.shape, 0) == iota(mark.shape, 1) // block, mark, 0), axis=0, keepdims=True)
    mark = mark * (2 * block) + block + iota((1, tokens), 1) % block
    take_new = (iota((rows, tokens), 0) == mark).astype(F32).astype(BF16)

    body = dot(take_read, keys) + dot(take_new, code)
    end = dot(take_read, key_tail) + dot(take_new, code_tail)
    end = end + jnp.where(iota(end.shape, 1) == rope, bias, 0.0)
    message[:, :, :width] = body.astype(BF16).reshape(count, 2 * block, width)
    message[:, :, width:] = end.astype(BF16).reshape(count, 2 * block, tail)


def shard_kernel(arrived, after_group, after_query, shard):
    count, double, width = arrived.shape
    block = double // 2
    shard[...] = arrived[...].astype(F32)[:, :block, :].reshape(count * block, width).astype(BF16)


def join_kernel(*refs):
    *pieces, out, done = refs
    rows = pieces[0].shape[0]
    for i, piece in enumerate(pieces):
        out[i * rows : (i + 1) * rows, :] = piece[...]
    done[...] = jnp.zeros_like(done)


def join(*pieces):
    rows, wide = pieces[0].shape
    return pl.pallas_call(
        join_kernel,
        in_specs=[VMEM] * len(pieces),
        out_specs=(VMEM, VMEM),
        out_shape=(
            jax.ShapeDtypeStruct((rows * len(pieces), wide), BF16),
            jax.ShapeDtypeStruct((8, LANES), F32),
        ),
        compiler_params=pltpu.CompilerParams(vmem_limit_bytes=2 * MIB),
    )(*pieces)


def gate_kernel(held, done, out):
    pass


def gate(held, done):
    return pl.pallas_call(
        gate_kernel,
        in_specs=[ANY, ANY],
        out_specs=ANY,
        out_shape=jax.ShapeDtypeStruct(held.shape, held.dtype),
        input_output_aliases={0: 0},
        compiler_params=pltpu.CompilerParams(vmem_limit_bytes=MIB),
    )(held, done)


def land_kernel(own_ref, column_ref, after, arrived, targets, slots, out_latent, out_rope, out_scale, done):
    done[...] = jnp.zeros_like(done)
    own, column = own_ref[0], column_ref[0]
    new, block, width = out_latent.shape
    count, double, _ = arrived.shape
    rope = out_rope.shape[1] // block
    tail = arrived.shape[2] - width

    def pick(table):
        return jnp.sum(jnp.where(iota(table.shape, 0) == column, table, 0), axis=0)

    target, slot = pick(targets[...]), pick(slots[...])
    cube = (new,) + target.shape
    hit = (jnp.broadcast_to(target[None], cube) == own) & (jnp.broadcast_to(slot[None], cube) == iota(cube, 0))
    source = jnp.sum(jnp.where(hit, iota(cube, 2), 0), axis=2, keepdims=True)
    source = jnp.sum(source, axis=1, keepdims=True)
    rows = new * block
    source = jnp.broadcast_to(source, (new, block, 1)).reshape(rows, 1)
    source = source * double + block + iota((rows, 1), 0) % block
    take = (iota((rows, count * double), 1) == source).astype(F32).astype(BF16)
    flat = arrived[...].reshape(count * double, width + tail)
    out_latent[...] = dot(take, flat[:, :width]).astype(BF16).reshape(new, block, width)
    end = dot(take, flat[:, width:])
    fold = fold_matrix(block, rope, tail)
    wide = dot_nt(end.astype(BF16), fold)
    wide = jnp.where(iota(wide.shape, 1) // rope == iota(wide.shape, 0) % block, wide, 0.0)
    out_rope[...] = jnp.sum(wide.reshape(new, block, block * rope), axis=1).astype(BF16)
    scale = jnp.sum(jnp.where(iota(end.shape, 1) == rope, end, 0.0), axis=1, keepdims=True)
    scale = jnp.broadcast_to(scale, (rows, block))
    scale = jnp.where(iota(scale.shape, 1) == iota(scale.shape, 0) % block, scale, 0.0)
    out_scale[...] = jnp.sum(scale.reshape(new, block, block), axis=1).astype(BF16)


def absorb_kernel(nope_hbm, rotary_hbm, weight_hbm, after, out, done, nope, rotary, weight, semaphores):
    done[...] = jnp.zeros_like(done)
    heads, depth, width = weight.shape
    tokens = nope.shape[0]
    rope = rotary.shape[1] // heads
    tail = out.shape[1] - width
    chunk = 8
    parts = [pl.ds(i * chunk, chunk) for i in range(heads // chunk)]
    copies = fetch(
        [nope_hbm, rotary_hbm] + [weight_hbm.at[p] for p in parts],
        [nope, rotary] + [weight.at[p] for p in parts],
        semaphores,
    )
    copies[0].wait()
    copies[1].wait()
    filler = (iota((tokens, tail - rope), 1) == 0).astype(F32).astype(BF16)
    for h in range(heads):
        if h % chunk == 0:
            copies[2 + h // chunk].wait()
        rows = slice(h * tokens, (h + 1) * tokens)
        out[rows, :width] = dot(nope[:, h * depth : (h + 1) * depth], weight[h]).astype(BF16)
        out[rows, width:] = jnp.concatenate([rotary[:, h * rope : (h + 1) * rope], filler], axis=1)


def attend_kernel(groups, blocks, first, last, sub, tokens, scale, *refs):
    refs = list(refs)
    query = refs.pop(0)
    if groups:
        group_ref = refs.pop(0)
    block_refs = [refs.pop(0) for _ in range(blocks)]
    if groups:
        column = refs.pop(0)[0]
    if not first:
        acc_in, top_in, total_in = refs.pop(0), refs.pop(0), refs.pop(0)
    if last:
        value, out = refs
    else:
        acc_out, top_out, total_out, done = refs
        done[...] = jnp.zeros_like(done)
    width = value.shape[1] if last else acc_out.shape[1]
    keys = [ref[...] for ref in block_refs]
    if groups:
        keys.insert(0, group_ref[...])
        ctx = group_ref.shape[0] // tokens
        core = lax.rem(column, 2)
        turn = 4 * core - 2
        order = [column, column + turn, column + 1 - 2 * core - turn, column + 2 * turn]
        order = [lax.rem(index + ctx, ctx) for index in order]
        order = [c for index in order for c in (index, index + 1 - 2 * core)]
        shape = (1, keys[0].shape[0])
        place = iota(shape, 1) % tokens
        for i, index in enumerate(order):
            place = place + jnp.where(iota(shape, 1) // tokens == i, index * tokens, 0)
        seen = place <= column * tokens + iota((sub, 1), 0) % tokens
    for part in range(query.shape[0] // sub):
        rows = slice(part * sub, (part + 1) * sub)
        q = query[rows, :]
        scores = [dot_nt(q, k) for k in keys]
        if groups:
            scores[0] = jnp.where(seen, scores[0], HIDDEN)
        top = functools.reduce(jnp.maximum, [jnp.max(s, axis=1, keepdims=True) for s in scores])
        weights = [jnp.exp((s - top) * scale) for s in scores]
        total = sum(jnp.sum(w, axis=1, keepdims=True) for w in weights)
        mixed = sum(dot(w.astype(BF16), k[:, :width]) for w, k in zip(weights, keys))
        top = jnp.broadcast_to(top, (sub, LANES))
        total = jnp.broadcast_to(total, (sub, LANES))
        if first:
            acc_out[rows, :] = mixed
            top_out[rows, :] = top
            total_out[rows, :] = total
            continue
        joint = jnp.maximum(top, top_in[rows, :])
        gain = jnp.exp((top - joint) * scale)
        fade = jnp.exp((top_in[rows, :] - joint) * scale)
        total = total * gain + total_in[rows, :] * fade
        if last:
            inverse = 1.0 / total
            gain, fade = gain * inverse, fade * inverse
        chunks = []
        for c in range(width // LANES):
            at = slice(c * LANES, (c + 1) * LANES)
            chunk = mixed[:, at] * gain + acc_in[rows, at] * fade
            if last:
                chunks.append(chunk.astype(BF16))
            else:
                acc_out[rows, at] = chunk
        if last:
            mixed = jnp.concatenate(chunks, axis=1)
            lanes = value.shape[2]
            for h in range(sub // tokens):
                head = part * (sub // tokens) + h
                out[:, head * lanes : (head + 1) * lanes] = dot(
                    mixed[h * tokens : (h + 1) * tokens], value[head]
                ).astype(BF16)
        else:
            top_out[rows, :] = joint
            total_out[rows, :] = total


def attend(query, blocks, tokens, width, scale, group=None, column=None, state=None, value=None, sub=1024):
    rows, wide = query.shape
    first, last = state is None, value is not None
    groups = group is not None
    operands = [query] + [group] * groups + list(blocks)
    specs = [VMEM] * len(operands)
    keys = sum(k.shape[0] for k in operands[1:])
    if groups:
        operands.append(column)
        specs.append(SMEM)
    if not first:
        operands += list(state)
        specs += [VMEM] * 3
    if last:
        operands.append(value)
        specs.append(VMEM)
        out_shape = jax.ShapeDtypeStruct((tokens, rows // tokens * value.shape[2]), BF16)
        out_specs = VMEM
    else:
        shapes = ((rows, width), (rows, LANES), (rows, LANES), (8, LANES))
        out_shape = tuple(jax.ShapeDtypeStruct(shape, F32) for shape in shapes)
        out_specs = (VMEM,) * 4
    return pl.pallas_call(
        functools.partial(attend_kernel, groups, len(blocks), first, last, sub, tokens, scale),
        in_specs=specs,
        out_specs=out_specs,
        out_shape=out_shape,
        compiler_params=pltpu.CompilerParams(vmem_limit_bytes=24 * MIB),
        cost_estimate=pl.CostEstimate(
            flops=2 * rows * keys * (wide + width), bytes_accessed=MIB, transcendentals=rows * keys
        ),
    )(*operands)


def body(
    query_nope,
    query_rope,
    suffix_latent,
    suffix_rope,
    absorb_key,
    absorb_value,
    pool_latent,
    pool_rope,
    pool_scale,
    prefix_tokens,
    block_owner,
    block_slot,
    write_owner,
    write_slot,
):
    own = lax.axis_index("pool")
    column = lax.axis_index("ctx")
    count = lax.axis_size("pool")
    ctx = lax.axis_size("ctx")
    heads, nope, latent = absorb_key.shape
    tokens = query_nope.shape[1]
    rope = query_rope.shape[2] // heads
    block = pool_scale.shape[3]
    slots = pool_scale.shape[2]
    new_blocks = write_owner.shape[2]
    wide = latent + 128
    scale = (nope + rope) ** -0.5
    own_at, column_at = own.reshape(1), column.reshape(1)
    ring = [(s, (s + (2 if s % 2 == 0 else -2)) % ctx) for s in range(ctx)]
    swap = [(s, s ^ 1) for s in range(ctx)]

    rows = slots * block
    targets, target_slots = jnp.transpose(write_owner, (1, 2, 0)), jnp.transpose(write_slot, (1, 2, 0))
    operands = (
        pool_latent[0, 0],
        pool_rope[0, 0],
        pool_scale[0, 0].T,
        suffix_latent[0],
        suffix_rope,
        prefix_tokens[None],
        block_owner,
        block_slot,
        targets,
    )
    message, suffix = pl.pallas_call(
        pack_kernel,
        in_specs=[SMEM, SMEM] + [HBM] * len(operands),
        out_specs=(VMEM, VMEM),
        out_shape=(
            jax.ShapeDtypeStruct((count, 2 * block, wide), BF16),
            jax.ShapeDtypeStruct((tokens, wide), BF16),
        ),
        scratch_shapes=[pltpu.VMEM(x.shape, x.dtype) for x in operands]
        + [pltpu.SemaphoreType.DMA((len(operands),))],
        compiler_params=pltpu.CompilerParams(vmem_limit_bytes=60 * MIB),
    )(own_at, column_at, *operands)
    arrived = lax.all_to_all(message, "pool", split_axis=0, concat_axis=0, tiled=True)

    pair, _ = join(suffix, lax.ppermute(suffix, "ctx", swap))
    pair_first = lax.ppermute(pair, "ctx", ring)
    operands = (query_nope[0], query_rope[0], absorb_key)
    query, query_done = pl.pallas_call(
        absorb_kernel,
        in_specs=[HBM] * 3 + [ANY],
        out_specs=(VMEM, VMEM),
        out_shape=(jax.ShapeDtypeStruct((heads * tokens, wide), BF16), jax.ShapeDtypeStruct((8, LANES), F32)),
        scratch_shapes=[pltpu.VMEM(x.shape, x.dtype) for x in operands]
        + [pltpu.SemaphoreType.DMA((2 + heads // 8,))],
        compiler_params=pltpu.CompilerParams(vmem_limit_bytes=16 * MIB),
        cost_estimate=pl.CostEstimate(
            flops=2 * heads * tokens * nope * latent, bytes_accessed=8 * MIB, transcendentals=0
        ),
    )(*operands, pair)

    pair_swap = lax.ppermute(pair_first, "ctx", swap)
    pair_far = lax.ppermute(pair_first, "ctx", ring)
    group, group_done = join(pair, pair_first, pair_swap, pair_far)

    shard = pl.pallas_call(
        shard_kernel,
        in_specs=[VMEM, ANY, ANY],
        out_specs=VMEM,
        out_shape=jax.ShapeDtypeStruct((rows, wide), BF16),
        compiler_params=pltpu.CompilerParams(vmem_limit_bytes=4 * MIB),
    )(arrived, group_done, query_done)

    run = functools.partial(attend, query, tokens=tokens, width=latent, scale=scale)
    sibling = lax.ppermute(shard, "ctx", swap)
    first = lax.ppermute(shard, "ctx", ring)
    second = lax.ppermute(sibling, "ctx", ring)
    *state, done = run([], group=group, column=column_at)
    first = gate(first, done)
    first_swap = lax.ppermute(first, "ctx", swap)
    third = lax.ppermute(first, "ctx", ring)
    *state, done = run([shard, sibling], state=state)
    written_latent, written_rope, written_scale, landed = pl.pallas_call(
        land_kernel,
        in_specs=[SMEM, SMEM, ANY] + [VMEM] * 3,
        out_specs=(VMEM,) * 4,
        out_shape=(
            jax.ShapeDtypeStruct((new_blocks, block, latent), BF16),
            jax.ShapeDtypeStruct((new_blocks, block * rope), BF16),
            jax.ShapeDtypeStruct((new_blocks, block), BF16),
            jax.ShapeDtypeStruct((8, LANES), F32),
        ),
        compiler_params=pltpu.CompilerParams(vmem_limit_bytes=8 * MIB),
    )(own_at, column_at, done, arrived, targets, target_slots)
    second = gate(second, landed)
    second_swap = lax.ppermute(second, "ctx", swap)
    *state, done = run([first, first_swap], state=state)
    third = gate(third, done)
    third_swap = lax.ppermute(third, "ctx", swap)
    *state, done = run([second, second_swap], state=state)
    attended = run([third, third_swap], state=state, value=absorb_value)
    return (attended[None], written_latent[None, None], written_rope[None, None], written_scale[None, None])


def solution(mesh):
    placed = (
        P("pool", "ctx", None),
        P("pool", "ctx", None),
        P("pool", "ctx", None),
        P("pool", "ctx"),
        P(),
        P(),
        P("pool", "ctx", None, None, None),
        P("pool", "ctx", None, None),
        P("pool", "ctx", None, None),
        P(),
        P(),
        P(),
        P(),
        P(),
    )
    return jax.shard_map(
        body,
        mesh=mesh,
        in_specs=placed,
        out_specs=(
            P("pool", "ctx", None),
            P("pool", "ctx", None, None, None),
            P("pool", "ctx", None, None),
            P("pool", "ctx", None, None),
        ),
        check_vma=False,
    )
```

```python
import functools
import math

import jax
import jax.numpy as jnp
from jax import lax
from jax.experimental import pallas as pl
from jax.experimental.pallas import tpu as pltpu
from jax.sharding import PartitionSpec as P

HIDDEN = -1e30
QUANT_TOP = 4.0
QUANT_EPS = 1e-06
MIB = 1 << 20
LANES = 128

F32 = jnp.float32
BF16 = jnp.bfloat16
VMEM = pl.BlockSpec(memory_space=pltpu.VMEM)
SMEM = pl.BlockSpec(memory_space=pltpu.SMEM)
ANY = pl.BlockSpec(memory_space=pl.ANY)
HBM = pl.BlockSpec(memory_space=pltpu.HBM)


def iota(shape, axis):
    return lax.broadcasted_iota(jnp.int32, shape, axis)


def dot(a, b):
    return jnp.dot(a, b, preferred_element_type=F32)


def dot_nt(a, b):
    return lax.dot_general(a, b, (((1,), (1,)), ((), ())), preferred_element_type=F32)


def fold_matrix(block, rope, lanes):
    shape = (block * rope, lanes)
    return (iota(shape, 0) % rope == iota(shape, 1)).astype(F32).astype(BF16)


def pick_column(table, column):
    return jnp.sum(jnp.where(iota(table.shape, 1) == column, table, 0), axis=1)


def fetch(sources, held, semaphores):
    copies = [
        pltpu.make_async_copy(source, target, semaphores.at[i])
        for i, (source, target) in enumerate(zip(sources, held))
    ]
    for copy in copies:
        copy.start()
    return copies


def pack_kernel(own_ref, column_ref, *refs):
    message, suffix, semaphores = refs[9], refs[10], refs[20]
    for copy in fetch(refs[:9], refs[11:20], semaphores):
        copy.wait()
    latent, ropes, scales, sfx_latent, sfx_rope, prefix, owners, slots, targets = refs[11:20]
    own, column = own_ref[0], column_ref[0]
    count, block, width = latent.shape
    rope = ropes.shape[1] // block
    ctx = owners.shape[1]
    tokens = sfx_latent.shape[0]
    tail = message.shape[2] - width
    rows = 2 * block * count
    fold = fold_matrix(block, rope, tail)

    cube = (count, block, count)
    factor = jnp.broadcast_to(scales[...].astype(F32)[None], cube)
    factor = jnp.sum(jnp.where(iota(cube, 0) == iota(cube, 2), factor, 0.0), axis=2, keepdims=True)
    keys = (latent[...].astype(F32) * factor).reshape(count * block, width).astype(BF16)
    wide = (count, block, block * rope)
    spread = jnp.broadcast_to(ropes[...].astype(F32)[:, None, :], wide) * factor
    spread = jnp.where(iota(wide, 2) // rope == iota(wide, 1), spread, 0.0)
    key_tail = dot(spread.reshape(count * block, block * rope).astype(BF16), fold).astype(BF16)

    own_latent = sfx_latent[...].astype(F32)
    pieces = []
    for g in range(tokens // block):
        piece = sfx_rope[:, g * block * rope : (g + 1) * block * rope].astype(F32)
        piece = jnp.broadcast_to(piece, (block, block * rope))
        pieces.append(jnp.where(iota(piece.shape, 1) // rope == iota(piece.shape, 0), piece, 0.0))
    own_tail = dot(jnp.concatenate(pieces, axis=0).astype(BF16), fold)
    suffix[:, :width] = sfx_latent[...]
    suffix[:, width:] = own_tail.astype(BF16)
    magnitude = jnp.maximum(
        jnp.max(jnp.abs(own_latent), axis=1, keepdims=True),
        jnp.max(jnp.abs(own_tail), axis=1, keepdims=True),
    )
    token_scale = ((magnitude + QUANT_EPS) / QUANT_TOP).astype(BF16).astype(F32)
    code = (own_latent / token_scale).astype(BF16)
    code_tail = jnp.where(iota(own_tail.shape, 1) == rope, token_scale, own_tail / token_scale)
    code_tail = code_tail.astype(BF16)

    def by_row(table):
        table = pick_column(table, column)[:, None, :]
        return jnp.broadcast_to(table, (count, 2 * block, table.shape[2])).reshape(rows, table.shape[2])

    mine = by_row(owners[...]) == own
    slot = jnp.sum(jnp.where(mine, by_row(slots[...]), 0), axis=1, keepdims=True)
    place = jnp.sum(jnp.where(mine, iota(mine.shape, 1), 0), axis=1, keepdims=True)
    unit = iota((rows, 1), 0) % (2 * block)
    limit_shape = (rows, count)
    limit = jnp.where(
        iota(limit_shape, 1) == iota(limit_shape, 0) // (2 * block),
        jnp.broadcast_to(prefix[...], limit_shape),
        0,
    )
    limit = jnp.sum(limit, axis=1, keepdims=True)
    read = unit < block
    bias = jnp.where(read & ((place * ctx + column) * block >= limit), HIDDEN, 0.0)
    source = jnp.where(read, slot * block + unit, -1)
    take_read = (iota((rows, count * block), 1) == source).astype(F32).astype(BF16)
    table = targets[...]
    mark = jnp.sum(jnp.where(iota(table.shape, 0) == column, table, 0), axis=0)
    mark = jnp.sum(jnp.where(iota(mark.shape, 1) == own, mark, 0), axis=1, keepdims=True)
    new = mark.shape[0]
    mark = jnp.broadcast_to(mark, (new, tokens))
    mark = jnp.sum(jnp.where(iota(mark.shape, 0) == iota(mark.shape, 1) // block, mark, 0), axis=0, keepdims=True)
    mark = mark * (2 * block) + block + iota((1, tokens), 1) % block
    take_new = (iota((rows, tokens), 0) == mark).astype(F32).astype(BF16)

    body = dot(take_read, keys) + dot(take_new, code)
    end = dot(take_read, key_tail) + dot(take_new, code_tail)
    end = end + jnp.where(iota(end.shape, 1) == rope, bias, 0.0)
    message[:, :, :width] = body.astype(BF16).reshape(count, 2 * block, width)
    message[:, :, width:] = end.astype(BF16).reshape(count, 2 * block, tail)


def shard_kernel(arrived, after_group, after_query, shard):
    count, double, width = arrived.shape
    block = double // 2
    shard[...] = arrived[...].astype(F32)[:, :block, :].reshape(count * block, width).astype(BF16)


def join_kernel(*refs):
    *pieces, out, done = refs
    rows = pieces[0].shape[0]
    for i, piece in enumerate(pieces):
        out[i * rows : (i + 1) * rows, :] = piece[...]
    done[...] = jnp.zeros_like(done)


def join(*pieces):
    rows, wide = pieces[0].shape
    return pl.pallas_call(
        join_kernel,
        in_specs=[VMEM] * len(pieces),
        out_specs=(VMEM, VMEM),
        out_shape=(
            jax.ShapeDtypeStruct((rows * len(pieces), wide), BF16),
            jax.ShapeDtypeStruct((8, LANES), F32),
        ),
        compiler_params=pltpu.CompilerParams(vmem_limit_bytes=2 * MIB),
    )(*pieces)


def gate_kernel(held, done, out):
    pass


def gate(held, done):
    return pl.pallas_call(
        gate_kernel,
        in_specs=[ANY, ANY],
        out_specs=ANY,
        out_shape=jax.ShapeDtypeStruct(held.shape, held.dtype),
        input_output_aliases={0: 0},
        compiler_params=pltpu.CompilerParams(vmem_limit_bytes=MIB),
    )(held, done)


def land_kernel(own_ref, column_ref, after, arrived, targets, slots, out_latent, out_rope, out_scale, done):
    done[...] = jnp.zeros_like(done)
    own, column = own_ref[0], column_ref[0]
    new, block, width = out_latent.shape
    count, double, _ = arrived.shape
    rope = out_rope.shape[1] // block
    tail = arrived.shape[2] - width

    def pick(table):
        return jnp.sum(jnp.where(iota(table.shape, 0) == column, table, 0), axis=0)

    target, slot = pick(targets[...]), pick(slots[...])
    cube = (new,) + target.shape
    hit = (jnp.broadcast_to(target[None], cube) == own) & (jnp.broadcast_to(slot[None], cube) == iota(cube, 0))
    source = jnp.sum(jnp.where(hit, iota(cube, 2), 0), axis=2, keepdims=True)
    source = jnp.sum(source, axis=1, keepdims=True)
    rows = new * block
    source = jnp.broadcast_to(source, (new, block, 1)).reshape(rows, 1)
    source = source * double + block + iota((rows, 1), 0) % block
    take = (iota((rows, count * double), 1) == source).astype(F32).astype(BF16)
    flat = arrived[...].reshape(count * double, width + tail)
    out_latent[...] = dot(take, flat[:, :width]).astype(BF16).reshape(new, block, width)
    end = dot(take, flat[:, width:])
    fold = fold_matrix(block, rope, tail)
    wide = dot_nt(end.astype(BF16), fold)
    wide = jnp.where(iota(wide.shape, 1) // rope == iota(wide.shape, 0) % block, wide, 0.0)
    out_rope[...] = jnp.sum(wide.reshape(new, block, block * rope), axis=1).astype(BF16)
    scale = jnp.sum(jnp.where(iota(end.shape, 1) == rope, end, 0.0), axis=1, keepdims=True)
    scale = jnp.broadcast_to(scale, (rows, block))
    scale = jnp.where(iota(scale.shape, 1) == iota(scale.shape, 0) % block, scale, 0.0)
    out_scale[...] = jnp.sum(scale.reshape(new, block, block), axis=1).astype(BF16)


def absorb_kernel(nope_hbm, rotary_hbm, weight_hbm, after, out, done, nope, rotary, weight, semaphores):
    done[...] = jnp.zeros_like(done)
    heads, depth, width = weight.shape
    tokens = nope.shape[0]
    rope = rotary.shape[1] // heads
    tail = out.shape[1] - width
    chunk = 8
    parts = [pl.ds(i * chunk, chunk) for i in range(heads // chunk)]
    copies = fetch(
        [nope_hbm, rotary_hbm] + [weight_hbm.at[p] for p in parts],
        [nope, rotary] + [weight.at[p] for p in parts],
        semaphores,
    )
    copies[0].wait()
    copies[1].wait()
    filler = (iota((tokens, tail - rope), 1) == 0).astype(F32).astype(BF16)
    for h in range(heads):
        if h % chunk == 0:
            copies[2 + h // chunk].wait()
        rows = slice(h * tokens, (h + 1) * tokens)
        out[rows, :width] = dot(nope[:, h * depth : (h + 1) * depth], weight[h]).astype(BF16)
        out[rows, width:] = jnp.concatenate([rotary[:, h * rope : (h + 1) * rope], filler], axis=1)


def attend_kernel(groups, blocks, first, last, sub, tokens, scale, *refs):
    refs = list(refs)
    query = refs.pop(0)
    if groups:
        group_ref = refs.pop(0)
    block_refs = [refs.pop(0) for _ in range(blocks)]
    if groups:
        column = refs.pop(0)[0]
    if not first:
        acc_in, top_in, total_in = refs.pop(0), refs.pop(0), refs.pop(0)
    if last:
        value, out = refs
    else:
        acc_out, top_out, total_out, done = refs
        done[...] = jnp.zeros_like(done)
    width = value.shape[1] if last else acc_out.shape[1]
    keys = [ref[...] for ref in block_refs]
    if groups:
        keys.insert(0, group_ref[...])
        ctx = group_ref.shape[0] // tokens
        core = lax.rem(column, 2)
        turn = 4 * core - 2
        order = [column, column + turn, column + 1 - 2 * core - turn, column + 2 * turn]
        order = [lax.rem(index + ctx, ctx) for index in order]
        order = [c for index in order for c in (index, index + 1 - 2 * core)]
        shape = (1, keys[0].shape[0])
        place = iota(shape, 1) % tokens
        for i, index in enumerate(order):
            place = place + jnp.where(iota(shape, 1) // tokens == i, index * tokens, 0)
        seen = place <= column * tokens + iota((sub, 1), 0) % tokens
    for part in range(query.shape[0] // sub):
        rows = slice(part * sub, (part + 1) * sub)
        q = query[rows, :]
        scores = [dot_nt(q, k) for k in keys]
        if groups:
            scores[0] = jnp.where(seen, scores[0], HIDDEN)
        top = functools.reduce(jnp.maximum, [jnp.max(s, axis=1, keepdims=True) for s in scores])
        weights = [jnp.exp2((s - top) * scale) for s in scores]
        total = sum(jnp.sum(w, axis=1, keepdims=True) for w in weights)
        mixed = sum(dot(w.astype(BF16), k[:, :width]) for w, k in zip(weights, keys))
        top = jnp.broadcast_to(top, (sub, LANES))
        total = jnp.broadcast_to(total, (sub, LANES))
        if first:
            acc_out[rows, :] = mixed
            top_out[rows, :] = top
            total_out[rows, :] = total
            continue
        joint = jnp.maximum(top, top_in[rows, :])
        gain = jnp.exp2((top - joint) * scale)
        fade = jnp.exp2((top_in[rows, :] - joint) * scale)
        total = total * gain + total_in[rows, :] * fade
        if last:
            inverse = 1.0 / total
            gain, fade = gain * inverse, fade * inverse
        chunks = []
        for c in range(width // LANES):
            at = slice(c * LANES, (c + 1) * LANES)
            chunk = mixed[:, at] * gain + acc_in[rows, at] * fade
            if last:
                chunks.append(chunk.astype(BF16))
            else:
                acc_out[rows, at] = chunk
        if last:
            mixed = jnp.concatenate(chunks, axis=1)
            lanes = value.shape[2]
            for h in range(sub // tokens):
                head = part * (sub // tokens) + h
                out[:, head * lanes : (head + 1) * lanes] = dot(
                    mixed[h * tokens : (h + 1) * tokens], value[head]
                ).astype(BF16)
        else:
            top_out[rows, :] = joint
            total_out[rows, :] = total


def attend(query, blocks, tokens, width, scale, group=None, column=None, state=None, value=None, sub=1024):
    rows, wide = query.shape
    first, last = state is None, value is not None
    groups = group is not None
    operands = [query] + [group] * groups + list(blocks)
    specs = [VMEM] * len(operands)
    keys = sum(k.shape[0] for k in operands[1:])
    if groups:
        operands.append(column)
        specs.append(SMEM)
    if not first:
        operands += list(state)
        specs += [VMEM] * 3
    if last:
        operands.append(value)
        specs.append(VMEM)
        out_shape = jax.ShapeDtypeStruct((tokens, rows // tokens * value.shape[2]), BF16)
        out_specs = VMEM
    else:
        shapes = ((rows, width), (rows, LANES), (rows, LANES), (8, LANES))
        out_shape = tuple(jax.ShapeDtypeStruct(shape, F32) for shape in shapes)
        out_specs = (VMEM,) * 4
    return pl.pallas_call(
        functools.partial(attend_kernel, groups, len(blocks), first, last, sub, tokens, scale),
        in_specs=specs,
        out_specs=out_specs,
        out_shape=out_shape,
        compiler_params=pltpu.CompilerParams(vmem_limit_bytes=24 * MIB),
        cost_estimate=pl.CostEstimate(
            flops=2 * rows * keys * (wide + width), bytes_accessed=MIB, transcendentals=rows * keys
        ),
    )(*operands)


def body(
    query_nope,
    query_rope,
    suffix_latent,
    suffix_rope,
    absorb_key,
    absorb_value,
    pool_latent,
    pool_rope,
    pool_scale,
    prefix_tokens,
    block_owner,
    block_slot,
    write_owner,
    write_slot,
):
    own = lax.axis_index("pool")
    column = lax.axis_index("ctx")
    count = lax.axis_size("pool")
    ctx = lax.axis_size("ctx")
    heads, nope, latent = absorb_key.shape
    tokens = query_nope.shape[1]
    rope = query_rope.shape[2] // heads
    block = pool_scale.shape[3]
    slots = pool_scale.shape[2]
    new_blocks = write_owner.shape[2]
    wide = latent + 128
    scale = (nope + rope) ** -0.5 * math.log2(math.e)
    own_at, column_at = own.reshape(1), column.reshape(1)
    ring = [(s, (s + (2 if s % 2 == 0 else -2)) % ctx) for s in range(ctx)]
    swap = [(s, s ^ 1) for s in range(ctx)]

    rows = slots * block
    targets, target_slots = jnp.transpose(write_owner, (1, 2, 0)), jnp.transpose(write_slot, (1, 2, 0))
    operands = (
        pool_latent[0, 0],
        pool_rope[0, 0],
        pool_scale[0, 0].T,
        suffix_latent[0],
        suffix_rope,
        prefix_tokens[None],
        block_owner,
        block_slot,
        targets,
    )
    message, suffix = pl.pallas_call(
        pack_kernel,
        in_specs=[SMEM, SMEM] + [HBM] * len(operands),
        out_specs=(VMEM, VMEM),
        out_shape=(
            jax.ShapeDtypeStruct((count, 2 * block, wide), BF16),
            jax.ShapeDtypeStruct((tokens, wide), BF16),
        ),
        scratch_shapes=[pltpu.VMEM(x.shape, x.dtype) for x in operands]
        + [pltpu.SemaphoreType.DMA((len(operands),))],
        compiler_params=pltpu.CompilerParams(vmem_limit_bytes=60 * MIB),
    )(own_at, column_at, *operands)
    arrived = lax.all_to_all(message, "pool", split_axis=0, concat_axis=0, tiled=True)

    pair, _ = join(suffix, lax.ppermute(suffix, "ctx", swap))
    pair_first = lax.ppermute(pair, "ctx", ring)
    operands = (query_nope[0], query_rope[0], absorb_key)
    query, query_done = pl.pallas_call(
        absorb_kernel,
        in_specs=[HBM] * 3 + [ANY],
        out_specs=(VMEM, VMEM),
        out_shape=(jax.ShapeDtypeStruct((heads * tokens, wide), BF16), jax.ShapeDtypeStruct((8, LANES), F32)),
        scratch_shapes=[pltpu.VMEM(x.shape, x.dtype) for x in operands]
        + [pltpu.SemaphoreType.DMA((2 + heads // 8,))],
        compiler_params=pltpu.CompilerParams(vmem_limit_bytes=16 * MIB),
        cost_estimate=pl.CostEstimate(
            flops=2 * heads * tokens * nope * latent, bytes_accessed=8 * MIB, transcendentals=0
        ),
    )(*operands, pair)

    pair_swap = lax.ppermute(pair_first, "ctx", swap)
    pair_far = lax.ppermute(pair_first, "ctx", ring)
    group, group_done = join(pair, pair_first, pair_swap, pair_far)

    shard = pl.pallas_call(
        shard_kernel,
        in_specs=[VMEM, ANY, ANY],
        out_specs=VMEM,
        out_shape=jax.ShapeDtypeStruct((rows, wide), BF16),
        compiler_params=pltpu.CompilerParams(vmem_limit_bytes=4 * MIB),
    )(arrived, group_done, query_done)

    run = functools.partial(attend, query, tokens=tokens, width=latent, scale=scale)
    sibling = lax.ppermute(shard, "ctx", swap)
    first = lax.ppermute(shard, "ctx", ring)
    second = lax.ppermute(sibling, "ctx", ring)
    *state, done = run([], group=group, column=column_at)
    first = gate(first, done)
    first_swap = lax.ppermute(first, "ctx", swap)
    third = lax.ppermute(first, "ctx", ring)
    *state, done = run([shard, sibling], state=state)
    written_latent, written_rope, written_scale, landed = pl.pallas_call(
        land_kernel,
        in_specs=[SMEM, SMEM, ANY] + [VMEM] * 3,
        out_specs=(VMEM,) * 4,
        out_shape=(
            jax.ShapeDtypeStruct((new_blocks, block, latent), BF16),
            jax.ShapeDtypeStruct((new_blocks, block * rope), BF16),
            jax.ShapeDtypeStruct((new_blocks, block), BF16),
            jax.ShapeDtypeStruct((8, LANES), F32),
        ),
        compiler_params=pltpu.CompilerParams(vmem_limit_bytes=8 * MIB),
    )(own_at, column_at, done, arrived, targets, target_slots)
    second = gate(second, landed)
    second_swap = lax.ppermute(second, "ctx", swap)
    *state, done = run([first, first_swap], state=state)
    third = gate(third, done)
    third_swap = lax.ppermute(third, "ctx", swap)
    *state, done = run([second, second_swap], state=state)
    attended = run([third, third_swap], state=state, value=absorb_value)
    return (attended[None], written_latent[None, None], written_rope[None, None], written_scale[None, None])


def solution(mesh):
    placed = (
        P("pool", "ctx", None),
        P("pool", "ctx", None),
        P("pool", "ctx", None),
        P("pool", "ctx"),
        P(),
        P(),
        P("pool", "ctx", None, None, None),
        P("pool", "ctx", None, None),
        P("pool", "ctx", None, None),
        P(),
        P(),
        P(),
        P(),
        P(),
    )
    return jax.shard_map(
        body,
        mesh=mesh,
        in_specs=placed,
        out_specs=(
            P("pool", "ctx", None),
            P("pool", "ctx", None, None, None),
            P("pool", "ctx", None, None),
            P("pool", "ctx", None, None),
        ),
        check_vma=False,
    )
```

```python
import functools
import math

import jax
import jax.numpy as jnp
from jax import lax
from jax.experimental import pallas as pl
from jax.experimental.pallas import tpu as pltpu
from jax.sharding import PartitionSpec as P

HIDDEN = -1e30
QUANT_TOP = 4.0
QUANT_EPS = 1e-06
MIB = 1 << 20
LANES = 128

F32 = jnp.float32
BF16 = jnp.bfloat16
VMEM = pl.BlockSpec(memory_space=pltpu.VMEM)
SMEM = pl.BlockSpec(memory_space=pltpu.SMEM)
ANY = pl.BlockSpec(memory_space=pl.ANY)
HBM = pl.BlockSpec(memory_space=pltpu.HBM)


def iota(shape, axis):
    return lax.broadcasted_iota(jnp.int32, shape, axis)


def dot(a, b):
    return jnp.dot(a, b, preferred_element_type=F32)


def dot_nt(a, b):
    return lax.dot_general(a, b, (((1,), (1,)), ((), ())), preferred_element_type=F32)


def fold_matrix(block, rope, lanes):
    shape = (block * rope, lanes)
    return (iota(shape, 0) % rope == iota(shape, 1)).astype(F32).astype(BF16)


def pick_column(table, column):
    return jnp.sum(jnp.where(iota(table.shape, 1) == column, table, 0), axis=1)


def fetch(sources, held, semaphores):
    copies = [
        pltpu.make_async_copy(source, target, semaphores.at[i])
        for i, (source, target) in enumerate(zip(sources, held))
    ]
    for copy in copies:
        copy.start()
    return copies


def pack_kernel(own_ref, column_ref, *refs):
    message, suffix, semaphores = refs[9], refs[10], refs[20]
    for copy in fetch(refs[:9], refs[11:20], semaphores):
        copy.wait()
    latent, ropes, scales, sfx_latent, sfx_rope, prefix, owners, slots, targets = refs[11:20]
    own, column = own_ref[0], column_ref[0]
    count, block, width = latent.shape
    rope = ropes.shape[1] // block
    ctx = owners.shape[1]
    tokens = sfx_latent.shape[0]
    tail = message.shape[2] - width
    rows = 2 * block * count
    fold = fold_matrix(block, rope, tail)

    cube = (count, block, count)
    factor = jnp.broadcast_to(scales[...].astype(F32)[None], cube)
    factor = jnp.sum(jnp.where(iota(cube, 0) == iota(cube, 2), factor, 0.0), axis=2, keepdims=True)
    keys = (latent[...].astype(F32) * factor).reshape(count * block, width).astype(BF16)
    wide = (count, block, block * rope)
    spread = jnp.broadcast_to(ropes[...].astype(F32)[:, None, :], wide) * factor
    spread = jnp.where(iota(wide, 2) // rope == iota(wide, 1), spread, 0.0)
    key_tail = dot(spread.reshape(count * block, block * rope).astype(BF16), fold).astype(BF16)

    own_latent = sfx_latent[...].astype(F32)
    pieces = []
    for g in range(tokens // block):
        piece = sfx_rope[:, g * block * rope : (g + 1) * block * rope].astype(F32)
        piece = jnp.broadcast_to(piece, (block, block * rope))
        pieces.append(jnp.where(iota(piece.shape, 1) // rope == iota(piece.shape, 0), piece, 0.0))
    own_tail = dot(jnp.concatenate(pieces, axis=0).astype(BF16), fold)
    suffix[:, :width] = sfx_latent[...]
    suffix[:, width:] = own_tail.astype(BF16)
    magnitude = jnp.maximum(
        jnp.max(jnp.abs(own_latent), axis=1, keepdims=True),
        jnp.max(jnp.abs(own_tail), axis=1, keepdims=True),
    )
    token_scale = ((magnitude + QUANT_EPS) / QUANT_TOP).astype(BF16).astype(F32)
    code = (own_latent / token_scale).astype(BF16)
    code_tail = jnp.where(iota(own_tail.shape, 1) == rope, token_scale, own_tail / token_scale)
    code_tail = code_tail.astype(BF16)

    def by_row(table):
        table = pick_column(table, column)[:, None, :]
        return jnp.broadcast_to(table, (count, 2 * block, table.shape[2])).reshape(rows, table.shape[2])

    mine = by_row(owners[...]) == own
    slot = jnp.sum(jnp.where(mine, by_row(slots[...]), 0), axis=1, keepdims=True)
    place = jnp.sum(jnp.where(mine, iota(mine.shape, 1), 0), axis=1, keepdims=True)
    unit = iota((rows, 1), 0) % (2 * block)
    limit_shape = (rows, count)
    limit = jnp.where(
        iota(limit_shape, 1) == iota(limit_shape, 0) // (2 * block),
        jnp.broadcast_to(prefix[...], limit_shape),
        0,
    )
    limit = jnp.sum(limit, axis=1, keepdims=True)
    read = unit < block
    bias = jnp.where(read & ((place * ctx + column) * block >= limit), HIDDEN, 0.0)
    source = jnp.where(read, slot * block + unit, -1)
    take_read = (iota((rows, count * block), 1) == source).astype(F32).astype(BF16)
    table = targets[...]
    mark = jnp.sum(jnp.where(iota(table.shape, 0) == column, table, 0), axis=0)
    mark = jnp.sum(jnp.where(iota(mark.shape, 1) == own, mark, 0), axis=1, keepdims=True)
    new = mark.shape[0]
    mark = jnp.broadcast_to(mark, (new, tokens))
    mark = jnp.sum(jnp.where(iota(mark.shape, 0) == iota(mark.shape, 1) // block, mark, 0), axis=0, keepdims=True)
    mark = mark * (2 * block) + block + iota((1, tokens), 1) % block
    take_new = (iota((rows, tokens), 0) == mark).astype(F32).astype(BF16)

    body = dot(take_read, keys) + dot(take_new, code)
    end = dot(take_read, key_tail) + dot(take_new, code_tail)
    end = end + jnp.where(iota(end.shape, 1) == rope, bias, 0.0)
    message[:, :, :width] = body.astype(BF16).reshape(count, 2 * block, width)
    message[:, :, width:] = end.astype(BF16).reshape(count, 2 * block, tail)


def shard_kernel(arrived, after_group, after_query, shard):
    count, double, width = arrived.shape
    block = double // 2
    shard[...] = arrived[...].astype(F32)[:, :block, :].reshape(count * block, width).astype(BF16)


def join_kernel(*refs):
    *pieces, out, done = refs
    rows = pieces[0].shape[0]
    for i, piece in enumerate(pieces):
        out[i * rows : (i + 1) * rows, :] = piece[...]
    done[...] = jnp.zeros_like(done)


def join(*pieces):
    rows, wide = pieces[0].shape
    return pl.pallas_call(
        join_kernel,
        in_specs=[VMEM] * len(pieces),
        out_specs=(VMEM, VMEM),
        out_shape=(
            jax.ShapeDtypeStruct((rows * len(pieces), wide), BF16),
            jax.ShapeDtypeStruct((8, LANES), F32),
        ),
        compiler_params=pltpu.CompilerParams(vmem_limit_bytes=2 * MIB),
    )(*pieces)


def gate_kernel(held, done, out):
    pass


def gate(held, done):
    return pl.pallas_call(
        gate_kernel,
        in_specs=[ANY, ANY],
        out_specs=ANY,
        out_shape=jax.ShapeDtypeStruct(held.shape, held.dtype),
        input_output_aliases={0: 0},
        compiler_params=pltpu.CompilerParams(vmem_limit_bytes=MIB),
    )(held, done)


def land_kernel(own_ref, column_ref, after, arrived, targets, slots, out_latent, out_rope, out_scale, done):
    done[...] = jnp.zeros_like(done)
    own, column = own_ref[0], column_ref[0]
    new, block, width = out_latent.shape
    count, double, _ = arrived.shape
    rope = out_rope.shape[1] // block
    tail = arrived.shape[2] - width

    def pick(table):
        return jnp.sum(jnp.where(iota(table.shape, 0) == column, table, 0), axis=0)

    target, slot = pick(targets[...]), pick(slots[...])
    cube = (new,) + target.shape
    hit = (jnp.broadcast_to(target[None], cube) == own) & (jnp.broadcast_to(slot[None], cube) == iota(cube, 0))
    source = jnp.sum(jnp.where(hit, iota(cube, 2), 0), axis=2, keepdims=True)
    source = jnp.sum(source, axis=1, keepdims=True)
    rows = new * block
    source = jnp.broadcast_to(source, (new, block, 1)).reshape(rows, 1)
    source = source * double + block + iota((rows, 1), 0) % block
    take = (iota((rows, count * double), 1) == source).astype(F32).astype(BF16)
    flat = arrived[...].reshape(count * double, width + tail)
    out_latent[...] = dot(take, flat[:, :width]).astype(BF16).reshape(new, block, width)
    end = dot(take, flat[:, width:])
    fold = fold_matrix(block, rope, tail)
    wide = dot_nt(end.astype(BF16), fold)
    wide = jnp.where(iota(wide.shape, 1) // rope == iota(wide.shape, 0) % block, wide, 0.0)
    out_rope[...] = jnp.sum(wide.reshape(new, block, block * rope), axis=1).astype(BF16)
    scale = jnp.sum(jnp.where(iota(end.shape, 1) == rope, end, 0.0), axis=1, keepdims=True)
    scale = jnp.broadcast_to(scale, (rows, block))
    scale = jnp.where(iota(scale.shape, 1) == iota(scale.shape, 0) % block, scale, 0.0)
    out_scale[...] = jnp.sum(scale.reshape(new, block, block), axis=1).astype(BF16)


def absorb_kernel(nope_hbm, rotary_hbm, weight_hbm, after, out, done, nope, rotary, weight, semaphores):
    done[...] = jnp.zeros_like(done)
    heads, depth, width = weight.shape
    tokens = nope.shape[0]
    rope = rotary.shape[1] // heads
    tail = out.shape[1] - width
    chunk = 8
    parts = [pl.ds(i * chunk, chunk) for i in range(heads // chunk)]
    copies = fetch(
        [nope_hbm, rotary_hbm] + [weight_hbm.at[p] for p in parts],
        [nope, rotary] + [weight.at[p] for p in parts],
        semaphores,
    )
    copies[0].wait()
    copies[1].wait()
    filler = (iota((tokens, tail - rope), 1) == 0).astype(F32).astype(BF16)
    for h in range(heads):
        if h % chunk == 0:
            copies[2 + h // chunk].wait()
        rows = slice(h * tokens, (h + 1) * tokens)
        out[rows, :width] = dot(nope[:, h * depth : (h + 1) * depth], weight[h]).astype(BF16)
        out[rows, width:] = jnp.concatenate([rotary[:, h * rope : (h + 1) * rope], filler], axis=1)


def attend_kernel(groups, blocks, first, last, sub, tokens, scale, *refs):
    refs = list(refs)
    query = refs.pop(0)
    if groups:
        group_ref = refs.pop(0)
    block_refs = [refs.pop(0) for _ in range(blocks)]
    if groups:
        column = refs.pop(0)[0]
    if not first:
        acc_in, top_in, total_in = refs.pop(0), refs.pop(0), refs.pop(0)
    if last:
        value, out = refs
    else:
        acc_out, top_out, total_out, done = refs
        done[...] = jnp.zeros_like(done)
    width = value.shape[1] if last else acc_out.shape[1]
    keys = [ref[...] for ref in block_refs]
    if groups:
        keys.insert(0, group_ref[...])
        ctx = group_ref.shape[0] // tokens
        core = lax.rem(column, 2)
        turn = 4 * core - 2
        order = [column, column + turn, column + 1 - 2 * core - turn, column + 2 * turn]
        order = [lax.rem(index + ctx, ctx) for index in order]
        order = [c for index in order for c in (index, index + 1 - 2 * core)]
        shape = (1, keys[0].shape[0])
        place = iota(shape, 1) % tokens
        for i, index in enumerate(order):
            place = place + jnp.where(iota(shape, 1) // tokens == i, index * tokens, 0)
        seen = place <= column * tokens + iota((sub, 1), 0) % tokens
    for part in range(query.shape[0] // sub):
        rows = slice(part * sub, (part + 1) * sub)
        q = query[rows, :]
        scores = [dot_nt(q, k) for k in keys]
        if groups:
            scores[0] = jnp.where(seen, scores[0], HIDDEN)
        top = functools.reduce(jnp.maximum, [jnp.max(s, axis=1, keepdims=True) for s in scores])
        weights = [jnp.exp2((s - top) * scale) for s in scores]
        total = sum(jnp.sum(w, axis=1, keepdims=True) for w in weights)
        mixed = sum(dot(w.astype(BF16), k[:, :width]) for w, k in zip(weights, keys))
        top = jnp.broadcast_to(top, (sub, LANES))
        total = jnp.broadcast_to(total, (sub, LANES))
        if first:
            acc_out[rows, :] = mixed
            top_out[rows, :] = top
            total_out[rows, :] = total
            continue
        joint = jnp.maximum(top, top_in[rows, :])
        gain = jnp.exp2((top - joint) * scale)
        fade = jnp.exp2((top_in[rows, :] - joint) * scale)
        total = total * gain + total_in[rows, :] * fade
        if last:
            inverse = 1.0 / total
            gain, fade = gain * inverse, fade * inverse
        chunks = []
        for c in range(width // LANES):
            at = slice(c * LANES, (c + 1) * LANES)
            chunk = mixed[:, at] * gain + acc_in[rows, at] * fade
            if last:
                chunks.append(chunk.astype(BF16))
            else:
                acc_out[rows, at] = chunk
        if last:
            mixed = jnp.concatenate(chunks, axis=1)
            lanes = value.shape[2]
            for h in range(sub // tokens):
                head = part * (sub // tokens) + h
                out[:, head * lanes : (head + 1) * lanes] = dot(
                    mixed[h * tokens : (h + 1) * tokens], value[head]
                ).astype(BF16)
        else:
            top_out[rows, :] = joint
            total_out[rows, :] = total


def attend(query, blocks, tokens, width, scale, group=None, column=None, state=None, value=None, sub=1024):
    rows, wide = query.shape
    first, last = state is None, value is not None
    groups = group is not None
    operands = [query] + [group] * groups + list(blocks)
    specs = [VMEM] * len(operands)
    keys = sum(k.shape[0] for k in operands[1:])
    if groups:
        operands.append(column)
        specs.append(SMEM)
    if not first:
        operands += list(state)
        specs += [VMEM] * 3
    if last:
        operands.append(value)
        specs.append(VMEM)
        out_shape = jax.ShapeDtypeStruct((tokens, rows // tokens * value.shape[2]), BF16)
        out_specs = VMEM
    else:
        shapes = ((rows, width), (rows, LANES), (rows, LANES), (8, LANES))
        out_shape = tuple(jax.ShapeDtypeStruct(shape, F32) for shape in shapes)
        out_specs = (VMEM,) * 4
    return pl.pallas_call(
        functools.partial(attend_kernel, groups, len(blocks), first, last, sub, tokens, scale),
        in_specs=specs,
        out_specs=out_specs,
        out_shape=out_shape,
        compiler_params=pltpu.CompilerParams(vmem_limit_bytes=24 * MIB),
        cost_estimate=pl.CostEstimate(
            flops=2 * rows * keys * (wide + width), bytes_accessed=MIB, transcendentals=rows * keys
        ),
    )(*operands)


def body(
    query_nope,
    query_rope,
    suffix_latent,
    suffix_rope,
    absorb_key,
    absorb_value,
    pool_latent,
    pool_rope,
    pool_scale,
    prefix_tokens,
    block_owner,
    block_slot,
    write_owner,
    write_slot,
):
    own = lax.axis_index("pool")
    column = lax.axis_index("ctx")
    count = lax.axis_size("pool")
    ctx = lax.axis_size("ctx")
    heads, nope, latent = absorb_key.shape
    tokens = query_nope.shape[1]
    rope = query_rope.shape[2] // heads
    block = pool_scale.shape[3]
    slots = pool_scale.shape[2]
    new_blocks = write_owner.shape[2]
    wide = latent + 128
    scale = (nope + rope) ** -0.5 * math.log2(math.e)
    own_at, column_at = own.reshape(1), column.reshape(1)
    ring = [(s, (s + (2 if s % 2 == 0 else -2)) % ctx) for s in range(ctx)]
    swap = [(s, s ^ 1) for s in range(ctx)]

    rows = slots * block
    targets, target_slots = jnp.transpose(write_owner, (1, 2, 0)), jnp.transpose(write_slot, (1, 2, 0))
    operands = (
        pool_latent[0, 0],
        pool_rope[0, 0],
        pool_scale[0, 0].T,
        suffix_latent[0],
        suffix_rope,
        prefix_tokens[None],
        block_owner,
        block_slot,
        targets,
    )
    message, suffix = pl.pallas_call(
        pack_kernel,
        in_specs=[SMEM, SMEM] + [HBM] * len(operands),
        out_specs=(VMEM, VMEM),
        out_shape=(
            jax.ShapeDtypeStruct((count, 2 * block, wide), BF16),
            jax.ShapeDtypeStruct((tokens, wide), BF16),
        ),
        scratch_shapes=[pltpu.VMEM(x.shape, x.dtype) for x in operands]
        + [pltpu.SemaphoreType.DMA((len(operands),))],
        compiler_params=pltpu.CompilerParams(vmem_limit_bytes=60 * MIB),
    )(own_at, column_at, *operands)
    arrived = lax.all_to_all(message, "pool", split_axis=0, concat_axis=0, tiled=True)

    near = lax.ppermute(suffix, "ctx", swap)
    chip = lax.ppermute(suffix, "ctx", ring)
    chip_near = lax.ppermute(near, "ctx", ring)
    far = lax.ppermute(chip, "ctx", ring)
    far_near = lax.ppermute(chip_near, "ctx", ring)
    pieces = [suffix, near, chip, chip_near]
    pieces += [lax.ppermute(piece, "ctx", swap) for piece in (chip, chip_near)]
    group, group_done = join(*pieces, far, far_near)
    operands = (query_nope[0], query_rope[0], absorb_key)
    query, query_done = pl.pallas_call(
        absorb_kernel,
        in_specs=[HBM] * 3 + [ANY],
        out_specs=(VMEM, VMEM),
        out_shape=(jax.ShapeDtypeStruct((heads * tokens, wide), BF16), jax.ShapeDtypeStruct((8, LANES), F32)),
        scratch_shapes=[pltpu.VMEM(x.shape, x.dtype) for x in operands]
        + [pltpu.SemaphoreType.DMA((2 + heads // 8,))],
        compiler_params=pltpu.CompilerParams(vmem_limit_bytes=16 * MIB),
        cost_estimate=pl.CostEstimate(
            flops=2 * heads * tokens * nope * latent, bytes_accessed=8 * MIB, transcendentals=0
        ),
    )(*operands, near)

    shard = pl.pallas_call(
        shard_kernel,
        in_specs=[VMEM, ANY, ANY],
        out_specs=VMEM,
        out_shape=jax.ShapeDtypeStruct((rows, wide), BF16),
        compiler_params=pltpu.CompilerParams(vmem_limit_bytes=4 * MIB),
    )(arrived, group_done, query_done)

    run = functools.partial(attend, query, tokens=tokens, width=latent, scale=scale)
    sibling = lax.ppermute(shard, "ctx", swap)
    first = lax.ppermute(shard, "ctx", ring)
    second = lax.ppermute(sibling, "ctx", ring)
    *state, done = run([], group=group, column=column_at)
    first = gate(first, done)
    first_swap = lax.ppermute(first, "ctx", swap)
    third = lax.ppermute(first, "ctx", ring)
    *state, done = run([shard, sibling], state=state)
    written_latent, written_rope, written_scale, landed = pl.pallas_call(
        land_kernel,
        in_specs=[SMEM, SMEM, ANY] + [VMEM] * 3,
        out_specs=(VMEM,) * 4,
        out_shape=(
            jax.ShapeDtypeStruct((new_blocks, block, latent), BF16),
            jax.ShapeDtypeStruct((new_blocks, block * rope), BF16),
            jax.ShapeDtypeStruct((new_blocks, block), BF16),
            jax.ShapeDtypeStruct((8, LANES), F32),
        ),
        compiler_params=pltpu.CompilerParams(vmem_limit_bytes=8 * MIB),
    )(own_at, column_at, done, arrived, targets, target_slots)
    second = gate(second, landed)
    second_swap = lax.ppermute(second, "ctx", swap)
    *state, done = run([first, first_swap], state=state)
    third = gate(third, done)
    third_swap = lax.ppermute(third, "ctx", swap)
    *state, done = run([second, second_swap], state=state)
    attended = run([third, third_swap], state=state, value=absorb_value)
    return (attended[None], written_latent[None, None], written_rope[None, None], written_scale[None, None])


def solution(mesh):
    placed = (
        P("pool", "ctx", None),
        P("pool", "ctx", None),
        P("pool", "ctx", None),
        P("pool", "ctx"),
        P(),
        P(),
        P("pool", "ctx", None, None, None),
        P("pool", "ctx", None, None),
        P("pool", "ctx", None, None),
        P(),
        P(),
        P(),
        P(),
        P(),
    )
    return jax.shard_map(
        body,
        mesh=mesh,
        in_specs=placed,
        out_specs=(
            P("pool", "ctx", None),
            P("pool", "ctx", None, None, None),
            P("pool", "ctx", None, None),
            P("pool", "ctx", None, None),
        ),
        check_vma=False,
    )
```
